32 devices in a mesh: seq: 8 (over z, y), head: 4 (over x, core).
Axes of the slice: x: 2, y: 2, z: 4, core: 2. Of those that a mesh axis runs over, the one named last changes fastest.
Arguments:
- qkv: bfloat16 [2, 3, 1024, 8, 128], P(None, None, 'seq', 'head'), may hold values from -48 to 48
- out_weight: bfloat16 [2, 8, 128, 2048], P(None, 'head'), may hold values from -0.59765625 to 0.59765625
- out_grad: bfloat16 [1024, 2048], P('seq', 'head'), may hold values from -6 to 6
Outputs:
- mixed: bfloat16 [1024, 2048], P('seq', 'head')
- grads: bfloat16 [2, 3, 1024, 8, 128], P(None, None, 'seq', 'head')
The draws below stay inside these ranges and needn't reach their ends.
All inputs are finite; a program needn't handle non-finite values.
Results may differ from the reference program's by a relative error of at most 0.039.
Values may be sent and summed in bfloat16 or wider, within the bound.
A program may use at most 64 MiB of HBM per device.

```python
import math
import jax
import jax.numpy as jnp
from jax import lax

HD = 128
HK = 8
D = 2048
ROW = 512
TOKENS = 1024


def draw_qkv(key, part):
    streams = jax.random.split(key, 1)
    shape = (2, 3, TOKENS, HK, HD)
    base = jnp.clip(jax.random.normal(streams[0], shape, jnp.float32), -4.0, 4.0)
    return base.astype(jnp.bfloat16)


def level_of(own_key, dims, shards, low, high):
    factor_of = 1.0
    for axis_at, parts in shards:
        draws = jax.random.uniform(jax.random.fold_in(jax.random.fold_in(own_key, 6), axis_at), (parts,), jnp.float32, low / len(shards), high / len(shards))
        factor_of = factor_of * jnp.repeat(jnp.exp(draws), dims[axis_at] // parts).reshape((-1,) + (1,) * (len(dims) - 1 - axis_at))
    return factor_of


def scatter_about(stream_key, extent, deviation, bound, shards=(), kind=jnp.bfloat16):
    gain = level_of(stream_key, extent, shards, -0.22, 0.18) if shards else 1.0
    drawn = jax.random.normal(stream_key, extent, jnp.float32) * deviation * gain
    return jnp.minimum(jnp.maximum(drawn, -bound), bound).astype(kind)


def setup_inputs(seed: int = 0) -> dict:
    key_list = jax.random.split(jax.random.key(seed), 4)
    return {
        "qkv": draw_qkv(jax.random.fold_in(key_list[3], 71), 0),
        "out_weight": scatter_about(key_list[1], (2, HK, HD, D), 0.1, 0.59765625, ((1, 4),)),
        "out_grad": scatter_about(key_list[2], (TOKENS, D), 1.0, 6.0, ((0, 8), (1, 4))),
    }


def rounded(values):
    return lax.optimization_barrier(values.astype(jnp.bfloat16)).astype(jnp.float32)

def masked_softmax(scores, allowed):
    largest = lax.optimization_barrier(jnp.max(jnp.where(allowed, scores, -jnp.inf), axis=-1, keepdims=True))
    raised = jnp.exp(jnp.where(allowed, scores - largest, -jnp.inf))
    totals = lax.optimization_barrier(jnp.sum(raised, axis=-1, keepdims=True))
    return (raised / totals, largest + jnp.log(totals))

def band_mask(query_pos, key_pos):
    apart = query_pos[:, None] - key_pos[None, :]
    return (apart >= 0) & (apart < ROW) & (key_pos[None, :] >= 0)

def reference(qkv, out_weight, out_grad):
    score_scale = 1.0 / math.sqrt(HD)
    line_count = TOKENS // ROW
    local_part = qkv[0].astype(jnp.float32)
    padded = jnp.pad(local_part[1:3], ((0, 0), (ROW, 0), (0, 0), (0, 0)))
    weight_full = out_weight.astype(jnp.float32)
    grad_heads = rounded(jnp.einsum('to,khdo->kthd', out_grad.astype(jnp.float32), weight_full))
    grad_local = grad_heads[0]

    def band_inputs(index):
        first = index * ROW
        query = lax.dynamic_slice_in_dim(local_part[0], first, ROW, 0)
        pairs = lax.dynamic_slice_in_dim(padded, first, 2 * ROW, 1)
        query_pos = first + jnp.arange(ROW, dtype=jnp.int32)
        key_pos = first - ROW + jnp.arange(2 * ROW, dtype=jnp.int32)
        scores = jnp.einsum('thd,shd->hts', query, pairs[0]) * score_scale
        return (query, pairs, scores, band_mask(query_pos, key_pos)[None])

    def band_forward(index):
        query, pairs, scores, allowed = band_inputs(index)
        weights, lse = masked_softmax(scores, allowed)
        attended = rounded(jnp.einsum('hts,shd->thd', rounded(weights), pairs[1]))
        return (attended, lse)
    indices = jnp.arange(line_count, dtype=jnp.int32)
    band_out, band_lse = lax.map(band_forward, indices)
    strided_part = qkv[1].astype(jnp.float32).reshape(3, line_count, ROW, HK, HD)
    line_idx = jnp.arange(line_count, dtype=jnp.int32)
    causal = line_idx[:, None] >= line_idx[None, :]
    col_scores = jnp.einsum('rchd,uchd->chru', strided_part[0], strided_part[1]) * score_scale
    col_weights, col_lse = masked_softmax(col_scores, causal)
    col_out = rounded(jnp.einsum('chru,uchd->rchd', rounded(col_weights), strided_part[2]))
    local_out = band_out.reshape(TOKENS, HK, HD)
    strided_out = col_out.reshape(TOKENS, HK, HD)
    mixed = (jnp.einsum('thd,hdo->to', local_out, weight_full[0]) + jnp.einsum('thd,hdo->to', strided_out, weight_full[1])).astype(jnp.bfloat16)

    def band_backward(index):
        query, pairs, scores, allowed = band_inputs(index)
        grad_o = lax.dynamic_slice_in_dim(grad_local, index * ROW, ROW, 0)
        attended = band_out[index]
        delta = jnp.einsum('thd,thd->ht', grad_o, attended)
        probs = jnp.exp(jnp.where(allowed, scores - band_lse[index], -jnp.inf))
        grad_p = jnp.einsum('thd,shd->hts', grad_o, pairs[1])
        grad_s = rounded(probs * (grad_p - delta[..., None]))
        grad_query = rounded(jnp.einsum('hts,shd->thd', grad_s, pairs[0]) * score_scale)
        grad_key = jnp.einsum('hts,thd->shd', grad_s, query) * score_scale
        grad_value = jnp.einsum('hts,thd->shd', rounded(probs), grad_o)
        return (grad_query, grad_key, grad_value)
    grad_query, grad_key, grad_value = lax.map(band_backward, indices)

    def combine(pieces):
        follow = jnp.concatenate([pieces[1:, :ROW], jnp.zeros_like(pieces[:1, :ROW])], axis=0)
        return (pieces[:, ROW:] + follow).reshape(TOKENS, HK, HD)
    local_grads = jnp.stack([grad_query.reshape(TOKENS, HK, HD), combine(grad_key), combine(grad_value)])
    grad_col = grad_heads[1].reshape(line_count, ROW, HK, HD)
    col_delta = jnp.einsum('rchd,rchd->chr', grad_col, col_out)
    col_probs = jnp.exp(jnp.where(causal, col_scores - col_lse, -jnp.inf))
    col_gp = jnp.einsum('rchd,uchd->chru', grad_col, strided_part[2])
    col_gs = rounded(col_probs * (col_gp - col_delta[..., None]))
    strided_dq = rounded(jnp.einsum('chru,uchd->rchd', col_gs, strided_part[1]) * score_scale)
    strided_dk = rounded(jnp.einsum('chru,rchd->uchd', col_gs, strided_part[0]) * score_scale)
    strided_dv = rounded(jnp.einsum('chru,rchd->uchd', rounded(col_probs), grad_col))
    strided_grads = jnp.stack([strided_dq, strided_dk, strided_dv]).reshape(3, TOKENS, HK, HD)
    grads = jnp.stack([local_grads.astype(jnp.bfloat16), strided_grads.astype(jnp.bfloat16)])
    return (mixed, grads)
```

```python
import functools
import math

import jax
import jax.numpy as jnp
from jax import lax
from jax.experimental import pallas as pl
from jax.experimental.pallas import tpu as pltpu
from jax.sharding import PartitionSpec as P

ROW = 512
MESH = pl.DeviceIdType.MESH
F32 = jnp.float32
BF16 = jnp.bfloat16


def dot_nn(a, b):
    return lax.dot_general(a, b, (((1,), (0,)), ((), ())), preferred_element_type=F32)


def dot_nt(a, b):
    return lax.dot_general(a, b, (((1,), (1,)), ((), ())), preferred_element_type=F32)


def dot_tn(a, b):
    return lax.dot_general(a, b, (((0,), (0,)), ((), ())), preferred_element_type=F32)


def layer_kernel(
    seq_count, head_groups, back, lines,
    qkv, w_hbm, og, mixed, grads,
    w, kvw, skv, ogf, dks, dkr, sdks, sdkr, mxs, mxr, dos, att, w_sem, ss, rs,
):
    r = lax.axis_index("seq")
    me = lax.axis_index("head")
    heads, shard, width = qkv.shape[2:]
    cols = og.shape[1]
    scale = 1.0 / math.sqrt(width)

    w_copy = pltpu.make_async_copy(w_hbm, w, w_sem)
    w_copy.start()

    spans = sorted(set(range(1, back + 1)) | {back * j for j in range(1, lines)})
    spans = [d for d in spans if d < seq_count]
    barrier = pltpu.get_barrier_semaphore()
    expected = jnp.int32(head_groups - 1)
    for d in spans:
        for target in (r + d, r - d):
            there = (target >= 0) & (target < seq_count)
            expected = expected + jnp.where(there, 1, 0)

            @pl.when(there)
            def _(target=target):
                pl.semaphore_signal(barrier, inc=1, device_id={"seq": target}, device_id_type=MESH)

    for k in range(1, head_groups):
        pl.semaphore_signal(
            barrier, inc=1, device_id={"head": lax.rem(me + k, head_groups)}, device_id_type=MESH
        )
    pl.semaphore_wait(barrier, expected)

    base = [0]

    def numbered(count):
        first = base[0]
        base[0] += count
        return first

    near = [d for d in range(1, back + 1) if d < seq_count]
    far = [j for j in range(1, lines)]
    og_at, kv_at, skv_at = numbered(head_groups), numbered(back + 1), numbered(lines)
    dk_at, sdk_at, mx_at = numbered(back + 1), numbered(lines), numbered(head_groups)

    def og_copy(k):
        return pltpu.make_async_remote_copy(
            src_ref=og, dst_ref=ogf.at[k - 1], send_sem=ss.at[og_at + k], recv_sem=rs.at[og_at + k],
            device_id={"head": lax.rem(me + k, head_groups)}, device_id_type=MESH,
        )

    def mx_copy(k):
        return pltpu.make_async_remote_copy(
            src_ref=mxs.at[k - 1], dst_ref=mxr.at[k - 1],
            send_sem=ss.at[mx_at + k], recv_sem=rs.at[mx_at + k],
            device_id={"head": lax.rem(me + k, head_groups)}, device_id_type=MESH,
        )

    def kv_copy(d):
        return pltpu.make_async_remote_copy(
            src_ref=qkv.at[0, 1:3], dst_ref=kvw.at[d - 1],
            send_sem=ss.at[kv_at + d], recv_sem=rs.at[kv_at + d],
            device_id={"seq": r + d}, device_id_type=MESH,
        )

    def skv_copy(j):
        return pltpu.make_async_remote_copy(
            src_ref=qkv.at[1, 1:3], dst_ref=skv.at[j - 1],
            send_sem=ss.at[skv_at + j], recv_sem=rs.at[skv_at + j],
            device_id={"seq": r + back * j}, device_id_type=MESH,
        )

    def dk_copy(d):
        return pltpu.make_async_remote_copy(
            src_ref=dks.at[d - 1], dst_ref=dkr.at[d - 1],
            send_sem=ss.at[dk_at + d], recv_sem=rs.at[dk_at + d],
            device_id={"seq": r - d}, device_id_type=MESH,
        )

    def sdk_copy(j):
        return pltpu.make_async_remote_copy(
            src_ref=sdks.at[j - 1], dst_ref=sdkr.at[j - 1],
            send_sem=ss.at[sdk_at + j], recv_sem=rs.at[sdk_at + j],
            device_id={"seq": r - back * j}, device_id_type=MESH,
        )

    def after(d):
        return r + d < seq_count

    def before(d):
        return r - d >= 0

    for k in range(1, head_groups):
        og_copy(k).start()
    for d in near:
        pl.when(after(d))(lambda d=d: kv_copy(d).start())
    for j in far:
        pl.when(after(back * j))(lambda j=j: skv_copy(j).start())
    for d in near:
        @pl.when(jnp.logical_not(before(d)))
        def _(d=d):
            kvw[d - 1] = jnp.zeros(kvw.shape[1:], BF16)
    for j in far:
        @pl.when(jnp.logical_not(before(back * j)))
        def _(j=j):
            skv[j - 1] = jnp.zeros(skv.shape[1:], BF16)

    w_copy.wait()

    def w_cols(group):
        return w[:, pl.ds(pl.multiple_of(group * cols, cols), cols)]

    total = dot_nt(og[...], w_cols(me))
    for k in range(1, head_groups):
        og_copy(k).wait_recv()
        total += dot_nt(ogf[k - 1], w_cols(lax.rem(me + head_groups - k, head_groups)))
    dos[...] = total.astype(BF16)

    for d in near:
        pl.when(before(d))(lambda d=d: kv_copy(d).wait_recv())
    row = lax.broadcasted_iota(jnp.int32, (shard, shard), 0)
    col = lax.broadcasted_iota(jnp.int32, (shard, shard), 1)
    allowed = []
    for d in [0] + near:
        apart = d * shard + row - col
        allowed.append((apart >= 0) & (apart < ROW) & before(d))
    allowed = jnp.concatenate(allowed, axis=1)
    own = []
    for h in range(heads):
        q = qkv[0, 0, h]
        keys = [qkv[0, 1, h]] + [kvw[d - 1, 0, h] for d in near]
        values = [qkv[0, 2, h]] + [kvw[d - 1, 1, h] for d in near]
        do = dos[:, h * width:(h + 1) * width]
        scores = jnp.concatenate([dot_nt(q, key) for key in keys], axis=1) * scale
        scores = jnp.where(allowed, scores, -jnp.inf)
        raised = jnp.exp(scores - jnp.max(scores, axis=1, keepdims=True))
        probs = raised / jnp.sum(raised, axis=1, keepdims=True)
        weights = probs.astype(BF16)
        parts = [weights[:, i * shard:(i + 1) * shard] for i in range(len(keys))]
        out = sum(dot_nn(p, v) for p, v in zip(parts, values)).astype(BF16)
        att[:, h * width:(h + 1) * width] = out
        delta = jnp.sum(do.astype(F32) * out.astype(F32), axis=1, keepdims=True)
        grad_p = jnp.concatenate([dot_nt(do, v) for v in values], axis=1)
        grad_s = (probs * (grad_p - delta)).astype(BF16)
        gs = [grad_s[:, i * shard:(i + 1) * shard] for i in range(len(keys))]
        grads[0, 0, h] = (sum(dot_nn(g, k) for g, k in zip(gs, keys)) * scale).astype(BF16)
        own.append((dot_tn(gs[0], q) * scale, dot_tn(parts[0], do)))
        for d in near:
            dks[d - 1, 0, h] = (dot_tn(gs[d], q) * scale).astype(BF16)
            dks[d - 1, 1, h] = dot_tn(parts[d], do).astype(BF16)
    for d in near:
        pl.when(before(d))(lambda d=d: dk_copy(d).start())

    for j in far:
        pl.when(before(back * j))(lambda j=j: skv_copy(j).wait_recv())
    strided_own = []
    for h in range(heads):
        q = qkv[1, 0, h].astype(F32)
        do = dos[:, (heads + h) * width:(heads + h + 1) * width].astype(F32)

        def key_of(j, h=h):
            return (qkv[1, 1, h] if j == 0 else skv[j - 1, 0, h]).astype(F32)

        def value_of(j, h=h):
            return (qkv[1, 2, h] if j == 0 else skv[j - 1, 1, h]).astype(F32)

        scores = [jnp.sum(q * key_of(0), axis=1, keepdims=True) * scale]
        for j in far:
            score = jnp.sum(q * key_of(j), axis=1, keepdims=True) * scale
            scores.append(jnp.where(before(back * j), score, -jnp.inf))
        largest = functools.reduce(jnp.maximum, scores)
        raised = [jnp.exp(s - largest) for s in scores]
        sums = sum(raised)
        probs = [e / sums for e in raised]
        rounded = [p.astype(BF16).astype(F32) for p in probs]
        out = sum(p * value_of(j) for j, p in enumerate(rounded)).astype(BF16)
        att[:, (heads + h) * width:(heads + h + 1) * width] = out
        delta = jnp.sum(do * out.astype(F32), axis=1, keepdims=True)
        grad_q = jnp.zeros_like(q)
        for j in [0] + far:
            grad_p = jnp.sum(do * value_of(j), axis=1, keepdims=True)
            grad_s = (probs[j] * (grad_p - delta)).astype(BF16).astype(F32)
            grad_q += grad_s * key_of(j)
            grad_k = grad_s * q * scale
            grad_v = rounded[j] * do
            if j == 0:
                strided_own.append((grad_k, grad_v))
            else:
                sdks[j - 1, 0, h] = grad_k.astype(BF16)
                sdks[j - 1, 1, h] = grad_v.astype(BF16)
        grads[1, 0, h] = (grad_q * scale).astype(BF16)
    for j in far:
        pl.when(before(back * j))(lambda j=j: sdk_copy(j).start())

    for k in range(1, head_groups):
        mxs[k - 1] = dot_nn(att[...], w_cols(lax.rem(me + k, head_groups))).astype(BF16)
        mx_copy(k).start()
    total = dot_nn(att[...], w_cols(me))

    for d in near:
        @pl.when(jnp.logical_not(after(d)))
        def _(d=d):
            dkr[d - 1] = jnp.zeros(dkr.shape[1:], BF16)

        pl.when(after(d))(lambda d=d: dk_copy(d).wait_recv())
    for h in range(heads):
        for i in range(2):
            grads[0, 1 + i, h] = (
                own[h][i] + sum(dkr[d - 1, i, h].astype(F32) for d in near)
            ).astype(BF16)
    for k in range(1, head_groups):
        mx_copy(k).wait_recv()
        total += mxr[k - 1].astype(F32)
    mixed[...] = total.astype(BF16)
    for j in far:
        @pl.when(jnp.logical_not(after(back * j)))
        def _(j=j):
            sdkr[j - 1] = jnp.zeros(sdkr.shape[1:], BF16)

        pl.when(after(back * j))(lambda j=j: sdk_copy(j).wait_recv())
    for h in range(heads):
        for i in range(2):
            grads[1, 1 + i, h] = (
                strided_own[h][i] + sum(sdkr[j - 1, i, h].astype(F32) for j in far)
            ).astype(BF16)

    for k in range(1, head_groups):
        og_copy(k).wait_send()
        mx_copy(k).wait_send()
    for d in near:
        pl.when(after(d))(lambda d=d: kv_copy(d).wait_send())
        pl.when(before(d))(lambda d=d: dk_copy(d).wait_send())
    for j in far:
        pl.when(after(back * j))(lambda j=j: skv_copy(j).wait_send())
        pl.when(before(back * j))(lambda j=j: sdk_copy(j).wait_send())


def shards(seq_count, head_groups, qkv, out_weight, out_grad):
    _, _, shard, heads, width = qkv.shape
    back = ROW // shard
    lines = seq_count * shard // ROW
    model = out_weight.shape[-1]
    cols = out_grad.shape[1]
    pairs = (2, heads, shard, width)
    copies = 2 * (head_groups + back + 1 + lines)
    vmem = pl.BlockSpec(memory_space=pltpu.VMEM)
    mixed, grads = pl.pallas_call(
        functools.partial(layer_kernel, seq_count, head_groups, back, lines),
        out_shape=[
            jax.ShapeDtypeStruct((shard, cols), BF16),
            jax.ShapeDtypeStruct((2, 3, heads, shard, width), BF16),
        ],
        in_specs=[vmem, pl.BlockSpec(memory_space=pl.ANY), vmem],
        out_specs=[vmem, vmem],
        scratch_shapes=[
            pltpu.VMEM((2 * heads * width, model), BF16),
            pltpu.VMEM((back,) + pairs, BF16),
            pltpu.VMEM((max(1, lines - 1),) + pairs, BF16),
            pltpu.VMEM((head_groups, shard, cols), BF16),
            pltpu.VMEM((back,) + pairs, BF16),
            pltpu.VMEM((back,) + pairs, BF16),
            pltpu.VMEM((max(1, lines - 1),) + pairs, BF16),
            pltpu.VMEM((max(1, lines - 1),) + pairs, BF16),
            pltpu.VMEM((head_groups, shard, cols), BF16),
            pltpu.VMEM((head_groups, shard, cols), BF16),
            pltpu.VMEM((shard, 2 * heads * width), BF16),
            pltpu.VMEM((shard, 2 * heads * width), BF16),
            pltpu.SemaphoreType.DMA,
            pltpu.SemaphoreType.DMA((copies,)),
            pltpu.SemaphoreType.DMA((copies,)),
        ],
        compiler_params=pltpu.CompilerParams(
            collective_id=0, has_side_effects=True, vmem_limit_bytes=48 * 1024 * 1024
        ),
    )(
        jnp.swapaxes(qkv, 2, 3),
        out_weight.reshape(2 * heads * width, model),
        out_grad,
    )
    return mixed, jnp.swapaxes(grads, 2, 3)


def solution(mesh):
    return jax.shard_map(
        functools.partial(shards, mesh.shape["seq"], mesh.shape["head"]),
        mesh=mesh,
        in_specs=(
            P(None, None, "seq", "head", None),
            P(None, "head", None, None),
            P("seq", "head"),
        ),
        out_specs=(P("seq", "head"), P(None, None, "seq", "head", None)),
        check_vma=False,
    )
```

```python
import functools
import math

import jax
import jax.numpy as jnp
from jax import lax
from jax.experimental import pallas as pl
from jax.experimental.pallas import tpu as pltpu
from jax.sharding import PartitionSpec as P

ROW = 512
MESH = pl.DeviceIdType.MESH
F32 = jnp.float32
BF16 = jnp.bfloat16


def dot_nn(a, b):
    return lax.dot_general(a, b, (((1,), (0,)), ((), ())), preferred_element_type=F32)


def dot_nt(a, b):
    return lax.dot_general(a, b, (((1,), (1,)), ((), ())), preferred_element_type=F32)


def dot_tn(a, b):
    return lax.dot_general(a, b, (((0,), (0,)), ((), ())), preferred_element_type=F32)


def layer_kernel(
    seq_count, head_groups, back, lines,
    qkv_hbm, w_hbm, og_hbm, mixed, grads,
    w, qkv, og, kvw, skv, ogf, even, odd, mate_in, up_out, up_in, sdks, sdkr, mxs, mxr, dos, att,
    in_sem, ss, rs,
):
    r = lax.axis_index("seq")
    me = lax.axis_index("head")
    heads, shard, width = qkv.shape[2:]
    cols = og.shape[1]
    scale = 1.0 / math.sqrt(width)
    side = lax.rem(r, 2)
    mate = r + 1 - 2 * side
    far = list(range(1, lines))
    steps = list(range(2, back + 1, 2))

    own_copy = pltpu.make_async_copy(
        qkv_hbm.at[0, 1:3], kvw.at[:, :, pl.ds(0, shard)], in_sem.at[0]
    )
    qkv_copy = pltpu.make_async_copy(qkv_hbm, qkv, in_sem.at[1])
    og_load = pltpu.make_async_copy(og_hbm, og, in_sem.at[2])
    w_copy = pltpu.make_async_copy(w_hbm, w, in_sem.at[3])
    for copy in (own_copy, og_load, qkv_copy, w_copy):
        copy.start()

    spans = sorted({2} | {back * j for j in far})
    barrier = pltpu.get_barrier_semaphore()
    expected = jnp.int32(head_groups)
    pl.semaphore_signal(barrier, inc=1, device_id={"seq": mate}, device_id_type=MESH)
    for k in range(1, head_groups):
        pl.semaphore_signal(
            barrier, inc=1, device_id={"head": lax.rem(me + k, head_groups)}, device_id_type=MESH
        )
    for d in spans:
        for target in (r + d, r - d):
            there = (target >= 0) & (target < seq_count)
            expected = expected + jnp.where(there, 1, 0)

            @pl.when(there)
            def _(target=target):
                pl.semaphore_signal(barrier, inc=1, device_id={"seq": target}, device_id_type=MESH)

    def after(d):
        return r + d < seq_count

    def before(d):
        return r - d >= 0

    def absent(there, ref):
        @pl.when(jnp.logical_not(there))
        def _():
            ref[...] = jnp.zeros(ref.shape, ref.dtype)

    def mate_sends(e):
        return before(e) & ((side == 1) if e == back else (side == 0) if e == 0 else True)

    def slot(d):
        return pl.ds(d * shard, shard)

    for d in range(1, back + 1):
        absent(before(d), kvw.at[:, :, slot(d)])
    for j in far:
        absent(before(back * j), skv.at[j - 1])
        absent(after(back * j), sdkr.at[j - 1])
    for e in [0] + steps:
        absent(mate_sends(e), mate_in.at[e // 2])
        if e < back:
            absent(after(2) & before(e), up_in.at[e // 2])

    base = [0]

    def numbered(count):
        first = base[0]
        base[0] += count
        return first

    og_at, mx_at = numbered(head_groups), numbered(head_groups)
    skv_at, sdk_at = numbered(lines), numbered(lines)
    kv_at, odd_at = numbered((back + 1) * heads), numbered((back + 1) * heads)
    up_at = numbered((back + 1) * heads)

    def remote(source, target, send_at, recv_at, device):
        return pltpu.make_async_remote_copy(
            src_ref=source, dst_ref=target, send_sem=ss.at[send_at], recv_sem=rs.at[recv_at],
            device_id=device, device_id_type=MESH,
        )

    def og_copy(k):
        device = {"head": lax.rem(me + k, head_groups)}
        return remote(og, ogf.at[k - 1], og_at + k, og_at + k, device)

    def mx_copy(k):
        device = {"head": lax.rem(me + k, head_groups)}
        return remote(mxs.at[k - 1], mxr.at[k - 1], mx_at + k, mx_at + k, device)

    def skv_copy(j):
        at = skv_at + j
        return remote(qkv.at[1, 1:3], skv.at[j - 1], at, at, {"seq": r + back * j})

    def sdk_copy(j):
        at = sdk_at + j
        return remote(sdks.at[j - 1], sdkr.at[j - 1], at, at, {"seq": r - back * j})

    def down_copy(d, h):
        at = kv_at + d * heads + h
        return remote(kvw.at[:, h, slot(d - 2)], kvw.at[:, h, slot(d)], at, at, {"seq": r + 2})

    def cross_copy(d, h):
        at = kv_at + d * heads + h
        source = pl.ds(pl.multiple_of((d - 1 + 2 * side) * shard, shard), shard)
        return remote(kvw.at[:, h, source], kvw.at[:, h, slot(d)], at, at, {"seq": mate})

    def pass_on(e, h):
        if e < back:
            pl.when(after(2) & before(e))(lambda: down_copy(e + 2, h).start())
            pl.when((side == 0) & before(e))(lambda: cross_copy(e + 1, h).start())
        if e > 0:
            pl.when((side == 1) & before(e))(lambda: cross_copy(e - 1, h).start())

    def odd_copy(d, h):
        into = (d + 1 - 2 * side) // 2
        at = odd_at + into * heads + h
        return remote(odd.at[d // 2, :, h], mate_in.at[into, :, h], odd_at + d * heads + h, at, {"seq": mate})

    def mate_wait(e, h):
        at = odd_at + (e // 2) * heads + h
        copy = remote(odd.at[0, :, h], mate_in.at[e // 2, :, h], at, at, {"seq": mate})
        pl.when(mate_sends(e))(lambda: copy.wait_recv())

    def up_copy(e, h):
        at = up_at + e * heads + h
        return remote(up_out.at[e // 2 - 1, :, h], up_in.at[e // 2 - 1, :, h], at, at, {"seq": r - 2})

    def gathered(e, h):
        mate_wait(e, h)
        total = even[e // 2, :, h] + mate_in[e // 2, :, h].astype(F32)
        if e < back:
            pl.when(after(2) & before(e))(lambda: up_copy(e + 2, h).wait_recv())
            total = total + up_in[e // 2, :, h].astype(F32)
        return total

    def send_up(e, h):
        up_out[e // 2 - 1, :, h] = gathered(e, h).astype(BF16)
        pl.when(before(e))(lambda: up_copy(e, h).start())

    own_copy.wait()
    pl.semaphore_wait(barrier, expected)
    for h in range(heads):
        pass_on(0, h)
    og_load.wait()
    for k in range(1, head_groups):
        og_copy(k).start()
    qkv_copy.wait()
    w_copy.wait()

    def w_cols(group):
        return w[:, pl.ds(pl.multiple_of(group * cols, cols), cols)]

    total = dot_nt(og[...], w_cols(me))
    for e in steps:
        for h in range(heads):
            pl.when(before(e))(lambda e=e, h=h: down_copy(e, h).wait_recv())
            pass_on(e, h)
    for j in far:
        pl.when(after(back * j))(lambda j=j: skv_copy(j).start())

    for k in range(1, head_groups):
        og_copy(k).wait_recv()
        total += dot_nt(ogf[k - 1], w_cols(lax.rem(me + head_groups - k, head_groups)))
    dos[...] = total.astype(BF16)

    window = (back + 1) * shard
    row = lax.broadcasted_iota(jnp.int32, (shard, window), 0)
    col = lax.broadcasted_iota(jnp.int32, (shard, window), 1)
    near = col // shard
    apart = near * shard + row - (col - near * shard)
    allowed = (apart >= 0) & (apart < ROW) & (near <= r)
    for h in range(heads):
        for d in range(1, back, 2):
            pl.when(before(d))(lambda d=d, h=h: cross_copy(d, h).wait_recv())
        q, keys, values = qkv[0, 0, h], kvw[0, h], kvw[1, h]
        do = dos[:, h * width:(h + 1) * width]
        scores = jnp.where(allowed, dot_nt(q, keys) * scale, -jnp.inf)
        raised = jnp.exp(scores - jnp.max(scores, axis=1, keepdims=True))
        probs = raised / jnp.sum(raised, axis=1, keepdims=True)
        weights = probs.astype(BF16)
        out = dot_nn(weights, values).astype(BF16)
        att[:, h * width:(h + 1) * width] = out
        delta = jnp.sum(do.astype(F32) * out.astype(F32), axis=1, keepdims=True)
        grad_s = (probs * (dot_nt(do, values) - delta)).astype(BF16)
        pair = (dot_tn(grad_s, q) * scale, dot_tn(weights, do))
        for i in range(2):
            for d in range(back + 1):
                part = pair[i][d * shard:(d + 1) * shard]
                if d % 2:
                    odd[d // 2, i, h] = part.astype(BF16)
                else:
                    even[d // 2, i, h] = part
        for d in reversed(range(1, back, 2)):
            pl.when(before(d))(lambda d=d, h=h: odd_copy(d, h).start())
        grads[0, 0, h] = (dot_nn(grad_s, keys) * scale).astype(BF16)
    for h in range(heads):
        send_up(back, h)

    for j in far:
        pl.when(before(back * j))(lambda j=j: skv_copy(j).wait_recv())

    def key_of(j, h):
        return (qkv[1, 1, h] if j == 0 else skv[j - 1, 0, h]).astype(F32)

    def value_of(j, h):
        return (qkv[1, 2, h] if j == 0 else skv[j - 1, 1, h]).astype(F32)

    strided_probs = []
    for h in range(heads):
        q = qkv[1, 0, h].astype(F32)
        scores = [jnp.sum(q * key_of(0, h), axis=1, keepdims=True) * scale]
        for j in far:
            score = jnp.sum(q * key_of(j, h), axis=1, keepdims=True) * scale
            scores.append(jnp.where(before(back * j), score, -jnp.inf))
        largest = functools.reduce(jnp.maximum, scores)
        raised = [jnp.exp(s - largest) for s in scores]
        sums = sum(raised)
        probs = [e / sums for e in raised]
        strided_probs.append(probs)
        out = sum(p.astype(BF16).astype(F32) * value_of(j, h) for j, p in enumerate(probs))
        att[:, (heads + h) * width:(heads + h + 1) * width] = out.astype(BF16)

    for k in range(1, head_groups):
        mxs[k - 1] = dot_nn(att[...], w_cols(lax.rem(me + k, head_groups))).astype(BF16)
        mx_copy(k).start()

    for e in reversed(steps[:-1]):
        for h in range(heads):
            send_up(e, h)

    strided_own = []
    for h in range(heads):
        lanes = slice((heads + h) * width, (heads + h + 1) * width)
        q, do = qkv[1, 0, h].astype(F32), dos[:, lanes].astype(F32)
        delta = jnp.sum(do * att[:, lanes].astype(F32), axis=1, keepdims=True)
        grad_q = jnp.zeros_like(q)
        for j in [0] + far:
            prob = strided_probs[h][j]
            grad_p = jnp.sum(do * value_of(j, h), axis=1, keepdims=True)
            grad_s = (prob * (grad_p - delta)).astype(BF16).astype(F32)
            grad_q += grad_s * key_of(j, h)
            grad_k = grad_s * q * scale
            grad_v = prob.astype(BF16).astype(F32) * do
            if j == 0:
                strided_own.append((grad_k, grad_v))
            else:
                sdks[j - 1, 0, h] = grad_k.astype(BF16)
                sdks[j - 1, 1, h] = grad_v.astype(BF16)
        grads[1, 0, h] = (grad_q * scale).astype(BF16)
    for j in far:
        pl.when(before(back * j))(lambda j=j: sdk_copy(j).start())

    total = dot_nn(att[...], w_cols(me))
    for h in range(heads):
        grads[0, 1:3, h] = gathered(0, h).astype(BF16)
    for k in range(1, head_groups):
        mx_copy(k).wait_recv()
        total += mxr[k - 1].astype(F32)
    mixed[...] = total.astype(BF16)
    for j in far:
        pl.when(after(back * j))(lambda j=j: sdk_copy(j).wait_recv())
    for h in range(heads):
        for i in range(2):
            grads[1, 1 + i, h] = (
                strided_own[h][i] + sum(sdkr[j - 1, i, h].astype(F32) for j in far)
            ).astype(BF16)

    for k in range(1, head_groups):
        og_copy(k).wait_send()
        mx_copy(k).wait_send()
    for h in range(heads):
        for e in [0] + steps:
            if e < back:
                pl.when(after(2) & before(e))(lambda e=e, h=h: down_copy(e + 2, h).wait_send())
            if e > 0:
                pl.when(before(e))(lambda e=e, h=h: up_copy(e, h).wait_send())
        for d in range(1, back, 2):
            pl.when(before(d - 1 + 2 * side))(lambda d=d, h=h: cross_copy(d, h).wait_send())
            pl.when(before(d))(lambda d=d, h=h: odd_copy(d, h).wait_send())
    for j in far:
        pl.when(after(back * j))(lambda j=j: skv_copy(j).wait_send())
        pl.when(before(back * j))(lambda j=j: sdk_copy(j).wait_send())


def shards(seq_count, head_groups, qkv, out_weight, out_grad):
    _, _, shard, heads, width = qkv.shape
    back = ROW // shard
    assert back * shard == ROW and back % 2 == 0 and seq_count % back == 0
    lines = seq_count // back
    others = max(1, lines - 1)
    model = out_weight.shape[-1]
    cols = out_grad.shape[1]
    pairs = (2, heads, shard, width)
    copies = 2 * (head_groups + lines) + 3 * (back + 1) * heads
    vmem = pl.BlockSpec(memory_space=pltpu.VMEM)
    hbm = pl.BlockSpec(memory_space=pl.ANY)
    mixed, grads = pl.pallas_call(
        functools.partial(layer_kernel, seq_count, head_groups, back, lines),
        out_shape=[
            jax.ShapeDtypeStruct((shard, cols), BF16),
            jax.ShapeDtypeStruct((2, 3, heads, shard, width), BF16),
        ],
        in_specs=[hbm, hbm, hbm],
        out_specs=[vmem, vmem],
        scratch_shapes=[
            pltpu.VMEM((2 * heads * width, model), BF16),
            pltpu.VMEM((2, 3, heads, shard, width), BF16),
            pltpu.VMEM((shard, cols), BF16),
            pltpu.VMEM((2, heads, (back + 1) * shard, width), BF16),
            pltpu.VMEM((others,) + pairs, BF16),
            pltpu.VMEM((head_groups, shard, cols), BF16),
            pltpu.VMEM((back // 2 + 1,) + pairs, F32),
            pltpu.VMEM((back // 2,) + pairs, BF16),
            pltpu.VMEM((back // 2 + 1,) + pairs, BF16),
            pltpu.VMEM((back // 2,) + pairs, BF16),
            pltpu.VMEM((back // 2,) + pairs, BF16),
            pltpu.VMEM((others,) + pairs, BF16),
            pltpu.VMEM((others,) + pairs, BF16),
            pltpu.VMEM((head_groups, shard, cols), BF16),
            pltpu.VMEM((head_groups, shard, cols), BF16),
            pltpu.VMEM((shard, 2 * heads * width), BF16),
            pltpu.VMEM((shard, 2 * heads * width), BF16),
            pltpu.SemaphoreType.DMA((4,)),
            pltpu.SemaphoreType.DMA((copies,)),
            pltpu.SemaphoreType.DMA((copies,)),
        ],
        compiler_params=pltpu.CompilerParams(
            collective_id=0, has_side_effects=True, vmem_limit_bytes=60 * 1024 * 1024
        ),
    )(
        jnp.swapaxes(qkv, 2, 3),
        out_weight.reshape(2 * heads * width, model),
        out_grad,
    )
    return mixed, jnp.swapaxes(grads, 2, 3)


def solution(mesh):
    return jax.shard_map(
        functools.partial(shards, mesh.shape["seq"], mesh.shape["head"]),
        mesh=mesh,
        in_specs=(
            P(None, None, "seq", "head", None),
            P(None, "head", None, None),
            P("seq", "head"),
        ),
        out_specs=(P("seq", "head"), P(None, None, "seq", "head", None)),
        check_vma=False,
    )
```

```python
import functools
import math

import jax
import jax.numpy as jnp
from jax import lax
from jax.experimental import pallas as pl
from jax.experimental.pallas import tpu as pltpu
from jax.sharding import PartitionSpec as P

ROW = 512
MESH = pl.DeviceIdType.MESH
F32 = jnp.float32
BF16 = jnp.bfloat16


def dot_nn(a, b):
    return lax.dot_general(a, b, (((1,), (0,)), ((), ())), preferred_element_type=F32)


def dot_nt(a, b):
    return lax.dot_general(a, b, (((1,), (1,)), ((), ())), preferred_element_type=F32)


def layer_kernel(
    seq_count, head_groups, back, lines, spans,
    qkv_hbm, w_hbm, og_hbm, mixed, grads,
    w, qkv, og, kvw, qw, dow, skv, sqw, sdow, ogf, mxs, mxr, att, stats, in_sem, ss, rs,
):
    r = lax.axis_index("seq")
    me = lax.axis_index("head")
    heads, shard, width = qkv.shape[2:]
    cols = og.shape[1]
    scale = 1.0 / math.sqrt(width)
    side = lax.rem(r, 2)
    mate = r + 1 - 2 * side
    far = list(range(1, lines))
    steps = list(range(2, back + 1, 2))

    def slot(d):
        return pl.ds(d * shard, shard)

    loads = [
        pltpu.make_async_copy(source, target, in_sem.at[i])
        for i, (source, target) in enumerate([
            (qkv_hbm.at[0, 1:3], kvw.at[:, :, slot(0)]),
            (qkv_hbm.at[0, 0], qw.at[:, slot(0)]),
            (og_hbm, og),
            (qkv_hbm, qkv),
            (w_hbm, w),
        ])
    ]
    for load in loads:
        load.start()

    turn = 1 - 2 * lax.rem(me, 2)
    partners = []
    for m in range(2, head_groups, 2):
        to, source = lax.rem(me + m, head_groups), lax.rem(me + head_groups - m, head_groups)
        partners += [(to, source), (to + turn, source + turn)]
    partners.append((me + turn, me + turn))

    barrier = pltpu.get_barrier_semaphore()
    expected = jnp.int32(head_groups - 1)
    for d in spans:
        for target in (r + d, r - d):
            there = (target >= 0) & (target < seq_count)
            expected = expected + jnp.where(there, 1, 0)

            @pl.when(there)
            def _(target=target):
                pl.semaphore_signal(barrier, inc=1, device_id={"seq": target}, device_id_type=MESH)
    for to, _ in partners:
        pl.semaphore_signal(barrier, inc=1, device_id={"head": to}, device_id_type=MESH)

    def after(d):
        return r + d < seq_count

    def before(d):
        return r - d >= 0

    def absent(there, *refs):
        @pl.when(jnp.logical_not(there))
        def _():
            for ref in refs:
                ref[...] = jnp.zeros(ref.shape, ref.dtype)

    for d in range(1, back + 1):
        absent(before(d), kvw.at[:, :, slot(d)])
        absent(after(d), qw.at[:, slot(d)], dow.at[:, slot(d)])
    for j in far:
        absent(before(back * j), skv.at[j - 1])
        absent(after(back * j), sqw.at[j - 1], sdow.at[j - 1])
    for i, d in enumerate(spans):
        absent(after(d), stats.at[i + 1])

    base = [0]

    def numbered(count):
        first = base[0]
        base[0] += count
        return first

    def remote(source, target, at, device):
        return pltpu.make_async_remote_copy(
            src_ref=source, dst_ref=target, send_sem=ss.at[at], recv_sem=rs.at[at],
            device_id=device, device_id_type=MESH,
        )

    class Cascade:
        def __init__(self, way, part):
            self.way, self.part = way, part
            self.rank = r if way == 1 else seq_count - 1 - r
            self.side = side if way == 1 else 1 - side
            self.at = numbered((back + 1) * heads)

        def has(self, d):
            return self.rank - d >= 0

        def onward(self, d, h):
            return remote(
                self.part(h, slot(d - 2)), self.part(h, slot(d)), self.at + d * heads + h,
                {"seq": r + 2 * self.way},
            )

        def across(self, d, h):
            source = pl.ds(pl.multiple_of((d - 1 + 2 * self.side) * shard, shard), shard)
            return remote(
                self.part(h, source), self.part(h, slot(d)), self.at + d * heads + h, {"seq": mate}
            )

        def goes_on(self, e):
            return (self.rank + 2 < seq_count) & self.has(e)

        def pass_on(self, e):
            for h in range(heads):
                if e:
                    pl.when(self.has(e))(lambda: self.onward(e, h).wait_recv())
                if e < back:
                    pl.when(self.goes_on(e))(lambda: self.onward(e + 2, h).start())
                    pl.when((self.side == 0) & self.has(e))(lambda: self.across(e + 1, h).start())
                if e:
                    pl.when((self.side == 1) & self.has(e))(lambda: self.across(e - 1, h).start())

        def finish(self, h):
            for d in range(1, back, 2):
                pl.when(self.has(d))(lambda: self.across(d, h).wait_recv())

        def sent(self):
            for h in range(heads):
                for e in [0] + steps[:-1]:
                    pl.when(self.goes_on(e))(lambda: self.onward(e + 2, h).wait_send())
                for d in range(1, back, 2):
                    pl.when(self.has(d - 1 + 2 * self.side))(lambda: self.across(d, h).wait_send())

    kv = Cascade(1, lambda h, rows: kvw.at[:, h, rows])
    query = Cascade(-1, lambda h, rows: qw.at[h, rows])
    cotangent = Cascade(-1, lambda h, rows: dow.at[h, rows])
    og_at, mx_at = numbered(head_groups), numbered(head_groups)
    skv_at, sq_at, sdo_at = numbered(lines), numbered(lines), numbered(lines)
    stat_at = numbered(len(spans))

    def og_copy(i):
        return remote(og, ogf.at[i], og_at + i, {"head": partners[i][0]})

    def mx_copy(i):
        return remote(mxs.at[i], mxr.at[i], mx_at + i, {"head": partners[i][0]})

    def skv_copy(j):
        return remote(qkv.at[1, 1:3], skv.at[j - 1], skv_at + j, {"seq": r + back * j})

    def sq_copy(j):
        return remote(qkv.at[1, 0], sqw.at[j - 1], sq_at + j, {"seq": r - back * j})

    def sdo_copy(j):
        return remote(sdow.at[lines - 1], sdow.at[j - 1], sdo_at + j, {"seq": r - back * j})

    def stat_copy(i):
        return remote(stats.at[0], stats.at[i + 1], stat_at + i, {"seq": r - spans[i]})

    for load in loads[:3]:
        load.wait()
    pl.semaphore_wait(barrier, expected)
    kv.pass_on(0)
    for i in range(len(partners)):
        og_copy(i).start()
    query.pass_on(0)
    for load in loads[3:]:
        load.wait()

    def w_cols(group):
        return w[:, pl.ds(pl.multiple_of(group * cols, cols), cols)]

    total = dot_nt(og[...], w_cols(me))
    for e in steps:
        kv.pass_on(e)
        query.pass_on(e)
    for j in far:
        pl.when(after(back * j))(lambda j=j: skv_copy(j).start())
        pl.when(before(back * j))(lambda j=j: sq_copy(j).start())

    for i in reversed(range(len(partners))):
        og_copy(i).wait_recv()
        total += dot_nt(ogf[i], w_cols(partners[i][1]))
    total = total.astype(BF16)
    for h in range(heads):
        dow[h, slot(0)] = total[:, h * width:(h + 1) * width]
        sdow[lines - 1, h] = total[:, (heads + h) * width:(heads + h + 1) * width]
    cotangent.pass_on(0)
    for j in far:
        pl.when(before(back * j))(lambda j=j: sdo_copy(j).start())

    window = (back + 1) * shard
    row = lax.broadcasted_iota(jnp.int32, (shard, window), 0)
    col = lax.broadcasted_iota(jnp.int32, (shard, window), 1)
    near = col // shard
    apart = near * shard + row - (col - near * shard)
    allowed = (apart >= 0) & (apart < ROW) & (near <= r)
    columns = [None] * (4 * heads)
    for h in range(heads):
        kv.finish(h)
        q, keys, values, do = qw[h, slot(0)], kvw[0, h], kvw[1, h], dow[h, slot(0)]
        scores = jnp.where(allowed, dot_nt(q, keys) * scale, -jnp.inf)
        largest = jnp.max(scores, axis=1, keepdims=True)
        raised = jnp.exp(scores - largest)
        sums = jnp.sum(raised, axis=1, keepdims=True)
        probs = raised / sums
        out = dot_nn(probs.astype(BF16), values).astype(BF16)
        att[:, h * width:(h + 1) * width] = out
        delta = jnp.sum(do.astype(F32) * out.astype(F32), axis=1, keepdims=True)
        columns[h], columns[heads + h] = largest + jnp.log(sums), delta
        grad_s = (probs * (dot_nt(do, values) - delta)).astype(BF16)
        grads[0, 0, h] = (dot_nn(grad_s, keys) * scale).astype(BF16)
        if h == 0:
            for e in steps[:-1]:
                cotangent.pass_on(e)

    for j in far:
        pl.when(before(back * j))(lambda j=j: skv_copy(j).wait_recv())

    def key_of(j, h):
        return (qkv[1, 1, h] if j == 0 else skv[j - 1, 0, h]).astype(F32)

    def value_of(j, h):
        return (qkv[1, 2, h] if j == 0 else skv[j - 1, 1, h]).astype(F32)

    strided_probs = []
    for h in range(heads):
        q, do = qkv[1, 0, h].astype(F32), sdow[lines - 1, h].astype(F32)
        scores = [jnp.sum(q * key_of(0, h), axis=1, keepdims=True) * scale]
        for j in far:
            score = jnp.sum(q * key_of(j, h), axis=1, keepdims=True) * scale
            scores.append(jnp.where(before(back * j), score, -jnp.inf))
        largest = functools.reduce(jnp.maximum, scores)
        raised = [jnp.exp(s - largest) for s in scores]
        sums = sum(raised)
        probs = [e / sums for e in raised]
        strided_probs.append(probs)
        out = sum(p.astype(BF16).astype(F32) * value_of(j, h) for j, p in enumerate(probs))
        out = out.astype(BF16)
        att[:, (heads + h) * width:(heads + h + 1) * width] = out
        columns[2 * heads + h] = largest + jnp.log(sums)
        columns[3 * heads + h] = jnp.sum(do * out.astype(F32), axis=1, keepdims=True)

    lane = lax.broadcasted_iota(jnp.int32, (shard, 128), 1)
    table = jnp.zeros((shard, 128), F32)
    for i, column in enumerate(columns):
        table = jnp.where(lane == i, column, table)
    stats[0] = table.T[:stats.shape[1]]
    for i, d in enumerate(spans):
        pl.when(before(d))(lambda i=i: stat_copy(i).start())

    for i, (to, _) in enumerate(partners):
        mxs[i] = dot_nn(att[...], w_cols(to)).astype(BF16)
        mx_copy(i).start()
    cotangent.pass_on(back)
    total = dot_nn(att[...], w_cols(me))

    strided = []
    for h in range(heads):
        q, do = qkv[1, 0, h].astype(F32), sdow[lines - 1, h].astype(F32)
        delta = columns[3 * heads + h]
        grad_q = jnp.zeros_like(q)
        for j in [0] + far:
            prob = strided_probs[h][j]
            grad_p = jnp.sum(do * value_of(j, h), axis=1, keepdims=True)
            grad_s = (prob * (grad_p - delta)).astype(BF16).astype(F32)
            grad_q += grad_s * key_of(j, h)
            if j == 0:
                strided.append((grad_s * q, prob.astype(BF16).astype(F32) * do))
        grads[1, 0, h] = (grad_q * scale).astype(BF16)

    for i, d in enumerate(spans):
        pl.when(after(d))(lambda i=i: stat_copy(i).wait_recv())
    apart = col - row
    allowed = (apart >= 0) & (apart < ROW) & (near < seq_count - r)
    later = [0] + [spans.index(d) + 1 for d in range(1, back + 1) if d in spans]
    later += [0] * (back + 1 - len(later))
    for h in range(heads):
        query.finish(h)
        cotangent.finish(h)
        queries, dos, key, value = qw[h], dow[h], kvw[0, h, slot(0)], kvw[1, h, slot(0)]
        lse = jnp.concatenate([stats[i, h:h + 1] for i in later], axis=1)
        delta = jnp.concatenate([stats[i, heads + h:heads + h + 1] for i in later], axis=1)
        probs = jnp.exp(jnp.where(allowed, dot_nt(key, queries) * scale - lse, -jnp.inf))
        grad_s = (probs * (dot_nt(value, dos) - delta)).astype(BF16)
        grads[0, 1, h] = (dot_nn(grad_s, queries) * scale).astype(BF16)
        grads[0, 2, h] = dot_nn(probs.astype(BF16), dos).astype(BF16)

    for j in far:
        @pl.when(after(back * j))
        def _(j=j):
            sq_copy(j).wait_recv()
            sdo_copy(j).wait_recv()
    for j in far:
        rows = stats[spans.index(back * j) + 1]
        table = jnp.concatenate([rows] * (128 // rows.shape[0]), axis=0).T
        for h in range(heads):
            q, do = sqw[j - 1, h].astype(F32), sdow[j - 1, h].astype(F32)
            lse = table[:, 2 * heads + h:2 * heads + h + 1]
            delta = table[:, 3 * heads + h:3 * heads + h + 1]
            score = jnp.sum(q * key_of(0, h), axis=1, keepdims=True) * scale
            prob = jnp.exp(jnp.where(after(back * j), score - lse, -jnp.inf))
            grad_p = jnp.sum(do * value_of(0, h), axis=1, keepdims=True)
            grad_s = (prob * (grad_p - delta)).astype(BF16).astype(F32)
            grad_k, grad_v = strided[h]
            strided[h] = (grad_k + grad_s * q, grad_v + prob.astype(BF16).astype(F32) * do)
    for h in range(heads):
        grads[1, 1, h] = (strided[h][0] * scale).astype(BF16)
        grads[1, 2, h] = strided[h][1].astype(BF16)

    for i in reversed(range(len(partners))):
        mx_copy(i).wait_recv()
        total += mxr[i].astype(F32)
    mixed[...] = total.astype(BF16)

    for i in range(len(partners)):
        og_copy(i).wait_send()
        mx_copy(i).wait_send()
    for cascade in (kv, query, cotangent):
        cascade.sent()
    for j in far:
        pl.when(after(back * j))(lambda j=j: skv_copy(j).wait_send())

        @pl.when(before(back * j))
        def _(j=j):
            sq_copy(j).wait_send()
            sdo_copy(j).wait_send()
    for i, d in enumerate(spans):
        pl.when(before(d))(lambda i=i: stat_copy(i).wait_send())


def shards(seq_count, head_groups, qkv, out_weight, out_grad):
    _, _, shard, heads, width = qkv.shape
    back = ROW // shard
    assert back * shard == ROW and back % 2 == 0 and seq_count % back == 0
    assert head_groups % 2 == 0
    lines = seq_count // back
    others = max(1, lines - 1)
    spans = [d for d in range(1, back + 1) if d < seq_count]
    spans += [back * j for j in range(2, lines)]
    model = out_weight.shape[-1]
    cols = out_grad.shape[1]
    window = (back + 1) * shard
    stat_rows = 4 * heads
    while 128 % stat_rows or stat_rows % 8:
        stat_rows += 1
    copies = 2 * head_groups + 3 * lines + 3 * (back + 1) * heads + len(spans)
    vmem = pl.BlockSpec(memory_space=pltpu.VMEM)
    hbm = pl.BlockSpec(memory_space=pltpu.HBM)
    mixed, grads = pl.pallas_call(
        functools.partial(layer_kernel, seq_count, head_groups, back, lines, spans),
        out_shape=[
            jax.ShapeDtypeStruct((shard, cols), BF16),
            jax.ShapeDtypeStruct((2, 3, heads, shard, width), BF16),
        ],
        in_specs=[pl.BlockSpec(memory_space=pl.ANY), hbm, hbm],
        out_specs=[vmem, vmem],
        scratch_shapes=[
            pltpu.VMEM((2 * heads * width, model), BF16),
            pltpu.VMEM((2, 3, heads, shard, width), BF16),
            pltpu.VMEM((shard, cols), BF16),
            pltpu.VMEM((2, heads, window, width), BF16),
            pltpu.VMEM((heads, window, width), BF16),
            pltpu.VMEM((heads, window, width), BF16),
            pltpu.VMEM((others, 2, heads, shard, width), BF16),
            pltpu.VMEM((others, heads, shard, width), BF16),
            pltpu.VMEM((lines, heads, shard, width), BF16),
            pltpu.VMEM((head_groups - 1, shard, cols), BF16),
            pltpu.VMEM((head_groups - 1, shard, cols), BF16),
            pltpu.VMEM((head_groups - 1, shard, cols), BF16),
            pltpu.VMEM((shard, 2 * heads * width), BF16),
            pltpu.VMEM((len(spans) + 1, stat_rows, shard), F32),
            pltpu.SemaphoreType.DMA((5,)),
            pltpu.SemaphoreType.DMA((copies,)),
            pltpu.SemaphoreType.DMA((copies,)),
        ],
        compiler_params=pltpu.CompilerParams(
            collective_id=0, has_side_effects=True, vmem_limit_bytes=40 * 1024 * 1024
        ),
    )(
        jnp.swapaxes(qkv, 2, 3),
        out_weight.reshape(2 * heads * width, model),
        out_grad,
    )
    return mixed, jnp.swapaxes(grads, 2, 3)


def solution(mesh):
    return jax.shard_map(
        functools.partial(shards, mesh.shape["seq"], mesh.shape["head"]),
        mesh=mesh,
        in_specs=(
            P(None, None, "seq", "head", None),
            P(None, "head", None, None),
            P("seq", "head"),
        ),
        out_specs=(P("seq", "head"), P(None, None, "seq", "head", None)),
        check_vma=False,
    )
```

```python
import functools
import math

import jax
import jax.numpy as jnp
from jax import lax
from jax.experimental import pallas as pl
from jax.experimental.pallas import tpu as pltpu
from jax.sharding import PartitionSpec as P

ROW = 512
MESH = pl.DeviceIdType.MESH
F32 = jnp.float32
BF16 = jnp.bfloat16


def dot_nn(a, b):
    return lax.dot_general(a, b, (((1,), (0,)), ((), ())), preferred_element_type=F32)


def dot_nt(a, b):
    return lax.dot_general(a, b, (((1,), (1,)), ((), ())), preferred_element_type=F32)


def layer_kernel(
    seq_count, head_groups, back, lines, spans,
    qkv_hbm, w_hbm, og_hbm, mixed, grads,
    w, qkv, og, kvw, qw, dow, skv, sqw, sdow, ogf, mxs, mxr, att, stats, in_sem, ss, rs,
):
    r = lax.axis_index("seq")
    me = lax.axis_index("head")
    heads, shard, width = qkv.shape[2:]
    cols = og.shape[1]
    scale = 1.0 / math.sqrt(width)
    side = lax.rem(r, 2)
    mate = r + 1 - 2 * side
    far = list(range(1, lines))
    steps = list(range(2, back + 1, 2))

    def slot(d):
        return pl.ds(d * shard, shard)

    loads = [
        pltpu.make_async_copy(source, target, in_sem.at[i])
        for i, (source, target) in enumerate([
            (qkv_hbm.at[0, 1:3], kvw.at[:, :, slot(0)]),
            (qkv_hbm.at[0, 0], qw.at[:, slot(0)]),
            (og_hbm, og),
            (qkv_hbm, qkv),
            (w_hbm, w),
        ])
    ]
    for load in loads:
        load.start()

    turn = 1 - 2 * lax.rem(me, 2)
    partners = []
    for m in range(2, head_groups, 2):
        to, source = lax.rem(me + m, head_groups), lax.rem(me + head_groups - m, head_groups)
        partners += [(to, source), (to + turn, source + turn)]
    partners.append((me + turn, me + turn))

    barrier = pltpu.get_barrier_semaphore()
    expected = jnp.int32(head_groups - 1)
    for d in spans:
        for target in (r + d, r - d):
            there = (target >= 0) & (target < seq_count)
            expected = expected + jnp.where(there, 1, 0)

            @pl.when(there)
            def _(target=target):
                pl.semaphore_signal(barrier, inc=1, device_id={"seq": target}, device_id_type=MESH)
    for to, _ in partners:
        pl.semaphore_signal(barrier, inc=1, device_id={"head": to}, device_id_type=MESH)

    def after(d):
        return r + d < seq_count

    def before(d):
        return r - d >= 0

    def absent(there, *refs):
        @pl.when(jnp.logical_not(there))
        def _():
            for ref in refs:
                ref[...] = jnp.zeros(ref.shape, ref.dtype)

    for d in range(1, back + 1):
        absent(before(d), kvw.at[:, :, slot(d)])
        absent(after(d), qw.at[:, slot(d)], dow.at[:, slot(d)])
    for j in far:
        absent(before(back * j), skv.at[j - 1])
        absent(after(back * j), sqw.at[j - 1], sdow.at[j - 1])
    for i, d in enumerate(spans):
        absent(after(d), stats.at[i + 1])

    base = [0]

    def numbered(count):
        first = base[0]
        base[0] += count
        return first

    def remote(source, target, at, device):
        return pltpu.make_async_remote_copy(
            src_ref=source, dst_ref=target, send_sem=ss.at[at], recv_sem=rs.at[at],
            device_id=device, device_id_type=MESH,
        )

    class Cascade:
        def __init__(self, way, part):
            self.way, self.part = way, part
            self.rank = r if way == 1 else seq_count - 1 - r
            self.side = side if way == 1 else 1 - side
            self.at = numbered((back + 1) * heads)

        def has(self, d):
            return self.rank - d >= 0

        def onward(self, d, h):
            return remote(
                self.part(h, slot(d - 2)), self.part(h, slot(d)), self.at + d * heads + h,
                {"seq": r + 2 * self.way},
            )

        def across(self, d, h):
            source = pl.ds(pl.multiple_of((d - 1 + 2 * self.side) * shard, shard), shard)
            return remote(
                self.part(h, source), self.part(h, slot(d)), self.at + d * heads + h, {"seq": mate}
            )

        def goes_on(self, e):
            return (self.rank + 2 < seq_count) & self.has(e)

        def pass_on(self, e):
            for h in range(heads):
                if e:
                    pl.when(self.has(e))(lambda: self.onward(e, h).wait_recv())
                if e < back:
                    pl.when(self.goes_on(e))(lambda: self.onward(e + 2, h).start())
                    pl.when((self.side == 0) & self.has(e))(lambda: self.across(e + 1, h).start())
                if e:
                    pl.when((self.side == 1) & self.has(e))(lambda: self.across(e - 1, h).start())

        def finish(self, h):
            for d in range(1, back, 2):
                pl.when(self.has(d))(lambda: self.across(d, h).wait_recv())

        def sent(self):
            for h in range(heads):
                for e in [0] + steps[:-1]:
                    pl.when(self.goes_on(e))(lambda: self.onward(e + 2, h).wait_send())
                for d in range(1, back, 2):
                    pl.when(self.has(d - 1 + 2 * self.side))(lambda: self.across(d, h).wait_send())

    kv = Cascade(1, lambda h, rows: kvw.at[:, h, rows])
    query = Cascade(-1, lambda h, rows: qw.at[h, rows])
    cotangent = Cascade(-1, lambda h, rows: dow.at[h, rows])
    og_at, mx_at = numbered(head_groups), numbered(head_groups)
    skv_at, sq_at, sdo_at = numbered(lines), numbered(lines), numbered(lines)
    stat_at = numbered(len(spans))

    def og_copy(i):
        return remote(og, ogf.at[i], og_at + i, {"head": partners[i][0]})

    def mx_copy(i):
        return remote(mxs.at[i], mxr.at[i], mx_at + i, {"head": partners[i][0]})

    def skv_copy(j):
        return remote(qkv.at[1, 1:3], skv.at[j - 1], skv_at + j, {"seq": r + back * j})

    def sq_copy(j):
        return remote(qkv.at[1, 0], sqw.at[j - 1], sq_at + j, {"seq": r - back * j})

    def sdo_copy(j):
        return remote(sdow.at[lines - 1], sdow.at[j - 1], sdo_at + j, {"seq": r - back * j})

    def stat_copy(i):
        return remote(stats.at[0], stats.at[i + 1], stat_at + i, {"seq": r - spans[i]})

    for load in loads[:3]:
        load.wait()
    pl.semaphore_wait(barrier, expected)
    kv.pass_on(0)
    for i in range(len(partners)):
        og_copy(i).start()
    query.pass_on(0)
    for load in loads[3:]:
        load.wait()

    def w_cols(group):
        return w[:, pl.ds(pl.multiple_of(group * cols, cols), cols)]

    total = dot_nt(og[...], w_cols(me))
    for e in steps:
        kv.pass_on(e)
        if e == steps[0]:
            for j in far:
                pl.when(after(back * j))(lambda j=j: skv_copy(j).start())
        query.pass_on(e)
    for j in far:
        pl.when(before(back * j))(lambda j=j: sq_copy(j).start())

    for i in reversed(range(len(partners))):
        og_copy(i).wait_recv()
        total += dot_nt(ogf[i], w_cols(partners[i][1]))
    total = total.astype(BF16)
    for h in range(heads):
        dow[h, slot(0)] = total[:, h * width:(h + 1) * width]
        sdow[lines - 1, h] = total[:, (heads + h) * width:(heads + h + 1) * width]
    cotangent.pass_on(0)
    for j in far:
        pl.when(before(back * j))(lambda j=j: sdo_copy(j).start())

    window = (back + 1) * shard
    row = lax.broadcasted_iota(jnp.int32, (shard, window), 0)
    col = lax.broadcasted_iota(jnp.int32, (shard, window), 1)
    near = col // shard
    apart = near * shard + row - (col - near * shard)
    allowed = (apart >= 0) & (apart < ROW) & (near <= r)
    columns = [None] * (4 * heads)
    local_probs = []
    for h in range(heads):
        kv.finish(h)
        q, keys, values = qw[h, slot(0)], kvw[0, h], kvw[1, h]
        scores = jnp.where(allowed, dot_nt(q, keys) * scale, -jnp.inf)
        largest = jnp.max(scores, axis=1, keepdims=True)
        raised = jnp.exp(scores - largest)
        sums = jnp.sum(raised, axis=1, keepdims=True)
        probs = raised / sums
        out = dot_nn(probs.astype(BF16), values).astype(BF16)
        att[:, h * width:(h + 1) * width] = out
        columns[h] = largest + jnp.log(sums)
        local_probs.append(probs)
        if h == 0:
            for e in steps[:-1]:
                cotangent.pass_on(e)

    for j in far:
        pl.when(before(back * j))(lambda j=j: skv_copy(j).wait_recv())

    def key_of(j, h):
        return (qkv[1, 1, h] if j == 0 else skv[j - 1, 0, h]).astype(F32)

    def value_of(j, h):
        return (qkv[1, 2, h] if j == 0 else skv[j - 1, 1, h]).astype(F32)

    strided_probs = []
    for h in range(heads):
        q = qkv[1, 0, h].astype(F32)
        scores = [jnp.sum(q * key_of(0, h), axis=1, keepdims=True) * scale]
        for j in far:
            score = jnp.sum(q * key_of(j, h), axis=1, keepdims=True) * scale
            scores.append(jnp.where(before(back * j), score, -jnp.inf))
        largest = functools.reduce(jnp.maximum, scores)
        raised = [jnp.exp(s - largest) for s in scores]
        sums = sum(raised)
        probs = [e / sums for e in raised]
        strided_probs.append(probs)
        out = sum(p.astype(BF16).astype(F32) * value_of(j, h) for j, p in enumerate(probs))
        att[:, (heads + h) * width:(heads + h + 1) * width] = out.astype(BF16)
        columns[2 * heads + h] = largest + jnp.log(sums)

    for i, (to, _) in enumerate(partners):
        mxs[i] = dot_nn(att[...], w_cols(to)).astype(BF16)
        mx_copy(i).start()
    cotangent.pass_on(back)

    for h in range(heads):
        for first, do in ((0, dow[h, slot(0)]), (heads, sdow[lines - 1, h])):
            out = att[:, (first + h) * width:(first + h + 1) * width]
            columns[2 * first + heads + h] = jnp.sum(
                do.astype(F32) * out.astype(F32), axis=1, keepdims=True
            )
    lane = lax.broadcasted_iota(jnp.int32, (shard, 128), 1)
    table = jnp.zeros((shard, 128), F32)
    for i, column in enumerate(columns):
        table = jnp.where(lane == i, column, table)
    stats[0] = table.T[:stats.shape[1]]
    for i, d in enumerate(spans):
        pl.when(before(d))(lambda i=i: stat_copy(i).start())

    for h in range(heads):
        grad_p = dot_nt(dow[h, slot(0)], kvw[1, h])
        grad_s = (local_probs[h] * (grad_p - columns[heads + h])).astype(BF16)
        grads[0, 0, h] = (dot_nn(grad_s, kvw[0, h]) * scale).astype(BF16)
    total = dot_nn(att[...], w_cols(me))

    strided = []
    for h in range(heads):
        q, do = qkv[1, 0, h].astype(F32), sdow[lines - 1, h].astype(F32)
        delta = columns[3 * heads + h]
        grad_q = jnp.zeros_like(q)
        for j in [0] + far:
            prob = strided_probs[h][j]
            grad_p = jnp.sum(do * value_of(j, h), axis=1, keepdims=True)
            grad_s = (prob * (grad_p - delta)).astype(BF16).astype(F32)
            grad_q += grad_s * key_of(j, h)
            if j == 0:
                strided.append((grad_s * q, prob.astype(BF16).astype(F32) * do))
        grads[1, 0, h] = (grad_q * scale).astype(BF16)

    for i, d in enumerate(spans):
        pl.when(after(d))(lambda i=i: stat_copy(i).wait_recv())
    apart = col - row
    allowed = (apart >= 0) & (apart < ROW) & (near < seq_count - r)
    later = [0] + [spans.index(d) + 1 for d in range(1, back + 1) if d in spans]
    later += [0] * (back + 1 - len(later))
    for h in range(heads):
        query.finish(h)
        cotangent.finish(h)
        queries, dos, key, value = qw[h], dow[h], kvw[0, h, slot(0)], kvw[1, h, slot(0)]
        lse = jnp.concatenate([stats[i, h:h + 1] for i in later], axis=1)
        delta = jnp.concatenate([stats[i, heads + h:heads + h + 1] for i in later], axis=1)
        probs = jnp.exp(jnp.where(allowed, dot_nt(key, queries) * scale - lse, -jnp.inf))
        grad_s = (probs * (dot_nt(value, dos) - delta)).astype(BF16)
        grads[0, 1, h] = (dot_nn(grad_s, queries) * scale).astype(BF16)
        grads[0, 2, h] = dot_nn(probs.astype(BF16), dos).astype(BF16)

    for j in far:
        @pl.when(after(back * j))
        def _(j=j):
            sq_copy(j).wait_recv()
            sdo_copy(j).wait_recv()
    for j in far:
        rows = stats[spans.index(back * j) + 1]
        table = jnp.concatenate([rows] * (128 // rows.shape[0]), axis=0).T
        for h in range(heads):
            q, do = sqw[j - 1, h].astype(F32), sdow[j - 1, h].astype(F32)
            lse = table[:, 2 * heads + h:2 * heads + h + 1]
            delta = table[:, 3 * heads + h:3 * heads + h + 1]
            score = jnp.sum(q * key_of(0, h), axis=1, keepdims=True) * scale
            prob = jnp.exp(jnp.where(after(back * j), score - lse, -jnp.inf))
            grad_p = jnp.sum(do * value_of(0, h), axis=1, keepdims=True)
            grad_s = (prob * (grad_p - delta)).astype(BF16).astype(F32)
            grad_k, grad_v = strided[h]
            strided[h] = (grad_k + grad_s * q, grad_v + prob.astype(BF16).astype(F32) * do)
    for h in range(heads):
        grads[1, 1, h] = (strided[h][0] * scale).astype(BF16)
        grads[1, 2, h] = strided[h][1].astype(BF16)

    for i in reversed(range(len(partners))):
        mx_copy(i).wait_recv()
        total += mxr[i].astype(F32)
    mixed[...] = total.astype(BF16)

    for i in range(len(partners)):
        og_copy(i).wait_send()
        mx_copy(i).wait_send()
    for cascade in (kv, query, cotangent):
        cascade.sent()
    for j in far:
        pl.when(after(back * j))(lambda j=j: skv_copy(j).wait_send())

        @pl.when(before(back * j))
        def _(j=j):
            sq_copy(j).wait_send()
            sdo_copy(j).wait_send()
    for i, d in enumerate(spans):
        pl.when(before(d))(lambda i=i: stat_copy(i).wait_send())


def shards(seq_count, head_groups, qkv, out_weight, out_grad):
    _, _, shard, heads, width = qkv.shape
    back = ROW // shard
    assert back * shard == ROW and back % 2 == 0 and seq_count % back == 0
    assert head_groups % 2 == 0
    lines = seq_count // back
    others = max(1, lines - 1)
    spans = [d for d in range(1, back + 1) if d < seq_count]
    spans += [back * j for j in range(2, lines)]
    model = out_weight.shape[-1]
    cols = out_grad.shape[1]
    window = (back + 1) * shard
    stat_rows = 4 * heads
    while 128 % stat_rows or stat_rows % 8:
        stat_rows += 1
    copies = 2 * head_groups + 3 * lines + 3 * (back + 1) * heads + len(spans)
    vmem = pl.BlockSpec(memory_space=pltpu.VMEM)
    hbm = pl.BlockSpec(memory_space=pltpu.HBM)
    mixed, grads = pl.pallas_call(
        functools.partial(layer_kernel, seq_count, head_groups, back, lines, spans),
        out_shape=[
            jax.ShapeDtypeStruct((shard, cols), BF16),
            jax.ShapeDtypeStruct((2, 3, heads, shard, width), BF16),
        ],
        in_specs=[pl.BlockSpec(memory_space=pl.ANY), hbm, hbm],
        out_specs=[vmem, vmem],
        scratch_shapes=[
            pltpu.VMEM((2 * heads * width, model), BF16),
            pltpu.VMEM((2, 3, heads, shard, width), BF16),
            pltpu.VMEM((shard, cols), BF16),
            pltpu.VMEM((2, heads, window, width), BF16),
            pltpu.VMEM((heads, window, width), BF16),
            pltpu.VMEM((heads, window, width), BF16),
            pltpu.VMEM((others, 2, heads, shard, width), BF16),
            pltpu.VMEM((others, heads, shard, width), BF16),
            pltpu.VMEM((lines, heads, shard, width), BF16),
            pltpu.VMEM((head_groups - 1, shard, cols), BF16),
            pltpu.VMEM((head_groups - 1, shard, cols), BF16),
            pltpu.VMEM((head_groups - 1, shard, cols), BF16),
            pltpu.VMEM((shard, 2 * heads * width), BF16),
            pltpu.VMEM((len(spans) + 1, stat_rows, shard), F32),
            pltpu.SemaphoreType.DMA((5,)),
            pltpu.SemaphoreType.DMA((copies,)),
            pltpu.SemaphoreType.DMA((copies,)),
        ],
        compiler_params=pltpu.CompilerParams(
            collective_id=0, has_side_effects=True, vmem_limit_bytes=52 * 1024 * 1024
        ),
    )(
        jnp.swapaxes(qkv, 2, 3),
        out_weight.reshape(2 * heads * width, model),
        out_grad,
    )
    return mixed, jnp.swapaxes(grads, 2, 3)


def solution(mesh):
    return jax.shard_map(
        functools.partial(shards, mesh.shape["seq"], mesh.shape["head"]),
        mesh=mesh,
        in_specs=(
            P(None, None, "seq", "head", None),
            P(None, "head", None, None),
            P("seq", "head"),
        ),
        out_specs=(P("seq", "head"), P(None, None, "seq", "head", None)),
        check_vma=False,
    )
```

```python
import functools
import math

import jax
import jax.numpy as jnp
from jax import lax
from jax.experimental import pallas as pl
from jax.experimental.pallas import tpu as pltpu
from jax.sharding import PartitionSpec as P

ROW = 512
MESH = pl.DeviceIdType.MESH
F32 = jnp.float32
BF16 = jnp.bfloat16


def dot_nn(a, b):
    return lax.dot_general(a, b, (((1,), (0,)), ((), ())), preferred_element_type=F32)


def dot_nt(a, b):
    return lax.dot_general(a, b, (((1,), (1,)), ((), ())), preferred_element_type=F32)


def layer_kernel(
    seq_count, head_groups, back, lines, spans,
    qkv_hbm, w_hbm, og_hbm, mixed, grads,
    w, qkv, og, kvw, qw, dow, skv, sqw, sdow, ogf, mxs, mxr, att, near_stats, far_stats, in_sem, ss, rs,
):
    r = lax.axis_index("seq")
    me = lax.axis_index("head")
    heads, shard, width = qkv.shape[2:]
    cols = og.shape[1]
    scale = 1.0 / math.sqrt(width)
    side = lax.rem(r, 2)
    mate = r + 1 - 2 * side
    far = list(range(1, lines))
    steps = list(range(2, back + 1, 2))

    def slot(d):
        return pl.ds(d * shard, shard)

    loads = [
        pltpu.make_async_copy(source, target, in_sem.at[i])
        for i, (source, target) in enumerate([
            (qkv_hbm.at[0, 1:3], kvw.at[:, :, slot(0)]),
            (qkv_hbm.at[0, 0], qw.at[:, slot(0)]),
            (og_hbm, og),
            (qkv_hbm, qkv),
            (w_hbm, w),
        ])
    ]
    for load in loads:
        load.start()

    turn = 1 - 2 * lax.rem(me, 2)
    partners = []
    for m in range(2, head_groups, 2):
        to, source = lax.rem(me + m, head_groups), lax.rem(me + head_groups - m, head_groups)
        partners += [(to, source), (to + turn, source + turn)]
    partners.append((me + turn, me + turn))

    barrier = pltpu.get_barrier_semaphore()
    expected = jnp.int32(head_groups - 1)
    for d in spans:
        for target in (r + d, r - d):
            there = (target >= 0) & (target < seq_count)
            expected = expected + jnp.where(there, 1, 0)

            @pl.when(there)
            def _(target=target):
                pl.semaphore_signal(barrier, inc=1, device_id={"seq": target}, device_id_type=MESH)
    for to, _ in partners:
        pl.semaphore_signal(barrier, inc=1, device_id={"head": to}, device_id_type=MESH)

    def after(d):
        return r + d < seq_count

    def before(d):
        return r - d >= 0

    def absent(there, *refs):
        @pl.when(jnp.logical_not(there))
        def _():
            for ref in refs:
                ref[...] = jnp.zeros(ref.shape, ref.dtype)

    for d in range(1, back + 1):
        absent(before(d), kvw.at[:, :, slot(d)])
        absent(after(d), qw.at[:, slot(d)], dow.at[:, slot(d)], near_stats.at[d])
    for j in far:
        absent(before(back * j), skv.at[j - 1])
        absent(after(back * j), sqw.at[j - 1], sdow.at[j - 1], far_stats.at[j])

    base = [0]

    def numbered(count):
        first = base[0]
        base[0] += count
        return first

    def remote(source, target, at, device):
        return pltpu.make_async_remote_copy(
            src_ref=source, dst_ref=target, send_sem=ss.at[at], recv_sem=rs.at[at],
            device_id=device, device_id_type=MESH,
        )

    class Cascade:
        def __init__(self, way, part):
            self.way, self.part = way, part
            self.rank = r if way == 1 else seq_count - 1 - r
            self.side = side if way == 1 else 1 - side
            self.at = numbered((back + 1) * heads)

        def has(self, d):
            return self.rank - d >= 0

        def onward(self, d, h):
            return remote(
                self.part(h, slot(d - 2)), self.part(h, slot(d)), self.at + d * heads + h,
                {"seq": r + 2 * self.way},
            )

        def across(self, d, h):
            source = pl.ds(pl.multiple_of((d - 1 + 2 * self.side) * shard, shard), shard)
            return remote(
                self.part(h, source), self.part(h, slot(d)), self.at + d * heads + h, {"seq": mate}
            )

        def goes_on(self, e):
            return (self.rank + 2 < seq_count) & self.has(e)

        def pass_on(self, e):
            for h in range(heads):
                if e:
                    pl.when(self.has(e))(lambda: self.onward(e, h).wait_recv())
                if e < back:
                    pl.when(self.goes_on(e))(lambda: self.onward(e + 2, h).start())
                    pl.when((self.side == 0) & self.has(e))(lambda: self.across(e + 1, h).start())
                if e:
                    pl.when((self.side == 1) & self.has(e))(lambda: self.across(e - 1, h).start())

        def finish(self, h):
            for d in range(1, back, 2):
                pl.when(self.has(d))(lambda: self.across(d, h).wait_recv())

        def sent(self):
            for h in range(heads):
                for e in [0] + steps[:-1]:
                    pl.when(self.goes_on(e))(lambda: self.onward(e + 2, h).wait_send())
                for d in range(1, back, 2):
                    pl.when(self.has(d - 1 + 2 * self.side))(lambda: self.across(d, h).wait_send())

    kv = Cascade(1, lambda h, rows: kvw.at[:, h, rows])
    query = Cascade(-1, lambda h, rows: qw.at[h, rows])
    cotangent = Cascade(-1, lambda h, rows: dow.at[h, rows])
    og_at, mx_at = numbered(head_groups), numbered(head_groups)
    skv_at, sq_at, sdo_at = numbered(lines), numbered(lines), numbered(lines)
    near_at, far_at = numbered(back + 1), numbered(lines)

    def og_copy(i):
        return remote(og, ogf.at[i], og_at + i, {"head": partners[i][0]})

    def mx_copy(i):
        return remote(mxs.at[i], mxr.at[i], mx_at + i, {"head": partners[i][0]})

    def skv_copy(j):
        return remote(qkv.at[1, 1:3], skv.at[j - 1], skv_at + j, {"seq": r + back * j})

    def sq_copy(j):
        return remote(qkv.at[1, 0], sqw.at[j - 1], sq_at + j, {"seq": r - back * j})

    def sdo_copy(j):
        return remote(sdow.at[lines - 1], sdow.at[j - 1], sdo_at + j, {"seq": r - back * j})

    def near_copy(d):
        return remote(near_stats.at[0], near_stats.at[d], near_at + d, {"seq": r - d})

    def far_copy(j):
        return remote(far_stats.at[0], far_stats.at[j], far_at + j, {"seq": r - back * j})

    def as_rows(columns):
        lane = lax.broadcasted_iota(jnp.int32, (shard, 128), 1)
        table = jnp.zeros((shard, 128), F32)
        for i, column in enumerate(columns):
            table = jnp.where(lane == i, column, table)
        return table.T[:near_stats.shape[1]]

    def delta_of(do, out):
        return jnp.sum(do.astype(F32) * out.astype(F32), axis=1, keepdims=True)

    for load in loads[:3]:
        load.wait()
    pl.semaphore_wait(barrier, expected)
    kv.pass_on(0)
    for i in range(len(partners)):
        og_copy(i).start()
    query.pass_on(0)
    for load in loads[3:]:
        load.wait()

    def w_cols(group):
        return w[:, pl.ds(pl.multiple_of(group * cols, cols), cols)]

    total = dot_nt(og[...], w_cols(me))
    for e in steps:
        kv.pass_on(e)
        query.pass_on(e)
    for j in far:
        pl.when(after(back * j))(lambda j=j: skv_copy(j).start())
        pl.when(before(back * j))(lambda j=j: sq_copy(j).start())

    for i in reversed(range(len(partners))):
        og_copy(i).wait_recv()
        total += dot_nt(ogf[i], w_cols(partners[i][1]))
    total = total.astype(BF16)
    for h in range(heads):
        dow[h, slot(0)] = total[:, h * width:(h + 1) * width]
        sdow[lines - 1, h] = total[:, (heads + h) * width:(heads + h + 1) * width]
    cotangent.pass_on(0)
    for j in far:
        pl.when(before(back * j))(lambda j=j: sdo_copy(j).start())

    window = (back + 1) * shard
    row = lax.broadcasted_iota(jnp.int32, (shard, window), 0)
    col = lax.broadcasted_iota(jnp.int32, (shard, window), 1)
    near = col // shard
    apart = near * shard + row - (col - near * shard)
    allowed = (apart >= 0) & (apart < ROW) & (near <= r)
    local_probs, lses, deltas = [], [], []
    for h in range(heads):
        kv.finish(h)
        q, keys, values = qw[h, slot(0)], kvw[0, h], kvw[1, h]
        scores = jnp.where(allowed, dot_nt(q, keys) * scale, -jnp.inf)
        largest = jnp.max(scores, axis=1, keepdims=True)
        raised = jnp.exp(scores - largest)
        sums = jnp.sum(raised, axis=1, keepdims=True)
        probs = raised / sums
        out = dot_nn(probs.astype(BF16), values).astype(BF16)
        att[:, h * width:(h + 1) * width] = out
        lses.append(largest + jnp.log(sums))
        deltas.append(delta_of(dow[h, slot(0)], out))
        local_probs.append(probs)
    near_stats[0] = as_rows(lses + deltas)
    for d in range(1, back + 1):
        pl.when(before(d))(lambda d=d: near_copy(d).start())
    for e in steps[:-1]:
        cotangent.pass_on(e)

    for j in far:
        pl.when(before(back * j))(lambda j=j: skv_copy(j).wait_recv())

    def key_of(j, h):
        return (qkv[1, 1, h] if j == 0 else skv[j - 1, 0, h]).astype(F32)

    def value_of(j, h):
        return (qkv[1, 2, h] if j == 0 else skv[j - 1, 1, h]).astype(F32)

    strided_probs, strided_lses, strided_deltas = [], [], []
    for h in range(heads):
        q = qkv[1, 0, h].astype(F32)
        scores = [jnp.sum(q * key_of(0, h), axis=1, keepdims=True) * scale]
        for j in far:
            score = jnp.sum(q * key_of(j, h), axis=1, keepdims=True) * scale
            scores.append(jnp.where(before(back * j), score, -jnp.inf))
        largest = functools.reduce(jnp.maximum, scores)
        raised = [jnp.exp(s - largest) for s in scores]
        sums = sum(raised)
        probs = [e / sums for e in raised]
        strided_probs.append(probs)
        out = sum(p.astype(BF16).astype(F32) * value_of(j, h) for j, p in enumerate(probs))
        out = out.astype(BF16)
        att[:, (heads + h) * width:(heads + h + 1) * width] = out
        strided_lses.append(largest + jnp.log(sums))
        strided_deltas.append(delta_of(sdow[lines - 1, h], out))
    far_stats[0] = as_rows(strided_lses + strided_deltas)
    for j in far:
        pl.when(before(back * j))(lambda j=j: far_copy(j).start())

    for i, (to, _) in enumerate(partners):
        mxs[i] = dot_nn(att[...], w_cols(to)).astype(BF16)
        mx_copy(i).start()
    cotangent.pass_on(back)

    for h in range(heads):
        grad_p = dot_nt(dow[h, slot(0)], kvw[1, h])
        grad_s = (local_probs[h] * (grad_p - deltas[h])).astype(BF16)
        grads[0, 0, h] = (dot_nn(grad_s, kvw[0, h]) * scale).astype(BF16)
    total = dot_nn(att[...], w_cols(me))

    strided = []
    for h in range(heads):
        q, do = qkv[1, 0, h].astype(F32), sdow[lines - 1, h].astype(F32)
        delta = strided_deltas[h]
        grad_q = jnp.zeros_like(q)
        for j in [0] + far:
            prob = strided_probs[h][j]
            grad_p = jnp.sum(do * value_of(j, h), axis=1, keepdims=True)
            grad_s = (prob * (grad_p - delta)).astype(BF16).astype(F32)
            grad_q += grad_s * key_of(j, h)
            if j == 0:
                strided.append((grad_s * q, prob.astype(BF16).astype(F32) * do))
        grads[1, 0, h] = (grad_q * scale).astype(BF16)

    for d in range(1, back + 1):
        pl.when(after(d))(lambda d=d: near_copy(d).wait_recv())
    apart = col - row
    allowed = (apart >= 0) & (apart < ROW) & (near < seq_count - r)
    for h in range(heads):
        query.finish(h)
        cotangent.finish(h)
        queries, dos, key, value = qw[h], dow[h], kvw[0, h, slot(0)], kvw[1, h, slot(0)]
        lse = jnp.concatenate([near_stats[d, h:h + 1] for d in range(back + 1)], axis=1)
        rows = [near_stats[d, heads + h:heads + h + 1] for d in range(back + 1)]
        delta = jnp.concatenate(rows, axis=1)
        probs = jnp.exp(jnp.where(allowed, dot_nt(key, queries) * scale - lse, -jnp.inf))
        grad_s = (probs * (dot_nt(value, dos) - delta)).astype(BF16)
        grads[0, 1, h] = (dot_nn(grad_s, queries) * scale).astype(BF16)
        grads[0, 2, h] = dot_nn(probs.astype(BF16), dos).astype(BF16)

    for j in far:
        @pl.when(after(back * j))
        def _(j=j):
            sq_copy(j).wait_recv()
            sdo_copy(j).wait_recv()
            far_copy(j).wait_recv()
    for j in far:
        rows = far_stats[j]
        table = jnp.concatenate([rows] * (128 // rows.shape[0]), axis=0).T
        for h in range(heads):
            q, do = sqw[j - 1, h].astype(F32), sdow[j - 1, h].astype(F32)
            lse = table[:, h:h + 1]
            delta = table[:, heads + h:heads + h + 1]
            score = jnp.sum(q * key_of(0, h), axis=1, keepdims=True) * scale
            prob = jnp.exp(jnp.where(after(back * j), score - lse, -jnp.inf))
            grad_p = jnp.sum(do * value_of(0, h), axis=1, keepdims=True)
            grad_s = (prob * (grad_p - delta)).astype(BF16).astype(F32)
            grad_k, grad_v = strided[h]
            strided[h] = (grad_k + grad_s * q, grad_v + prob.astype(BF16).astype(F32) * do)
    for h in range(heads):
        grads[1, 1, h] = (strided[h][0] * scale).astype(BF16)
        grads[1, 2, h] = strided[h][1].astype(BF16)

    for i in reversed(range(len(partners))):
        mx_copy(i).wait_recv()
        total += mxr[i].astype(F32)
    mixed[...] = total.astype(BF16)

    for i in range(len(partners)):
        og_copy(i).wait_send()
        mx_copy(i).wait_send()
    for cascade in (kv, query, cotangent):
        cascade.sent()
    for j in far:
        pl.when(after(back * j))(lambda j=j: skv_copy(j).wait_send())

        @pl.when(before(back * j))
        def _(j=j):
            sq_copy(j).wait_send()
            sdo_copy(j).wait_send()
            far_copy(j).wait_send()
    for d in range(1, back + 1):
        pl.when(before(d))(lambda d=d: near_copy(d).wait_send())


def shards(seq_count, head_groups, qkv, out_weight, out_grad):
    _, _, shard, heads, width = qkv.shape
    back = ROW // shard
    assert back * shard == ROW and back % 2 == 0 and seq_count % back == 0
    assert head_groups % 2 == 0
    lines = seq_count // back
    others = max(1, lines - 1)
    spans = list(range(1, back + 1))
    spans += [back * j for j in range(2, lines)]
    model = out_weight.shape[-1]
    cols = out_grad.shape[1]
    window = (back + 1) * shard
    stat_rows = 2 * heads
    while 128 % stat_rows or stat_rows % 8:
        stat_rows += 1
    copies = 2 * head_groups + 3 * lines + 3 * (back + 1) * heads + back + 1 + lines
    vmem = pl.BlockSpec(memory_space=pltpu.VMEM)
    hbm = pl.BlockSpec(memory_space=pltpu.HBM)
    mixed, grads = pl.pallas_call(
        functools.partial(layer_kernel, seq_count, head_groups, back, lines, spans),
        out_shape=[
            jax.ShapeDtypeStruct((shard, cols), BF16),
            jax.ShapeDtypeStruct((2, 3, heads, shard, width), BF16),
        ],
        in_specs=[pl.BlockSpec(memory_space=pl.ANY), hbm, hbm],
        out_specs=[vmem, vmem],
        scratch_shapes=[
            pltpu.VMEM((2 * heads * width, model), BF16),
            pltpu.VMEM((2, 3, heads, shard, width), BF16),
            pltpu.VMEM((shard, cols), BF16),
            pltpu.VMEM((2, heads, window, width), BF16),
            pltpu.VMEM((heads, window, width), BF16),
            pltpu.VMEM((heads, window, width), BF16),
            pltpu.VMEM((others, 2, heads, shard, width), BF16),
            pltpu.VMEM((others, heads, shard, width), BF16),
            pltpu.VMEM((lines, heads, shard, width), BF16),
            pltpu.VMEM((head_groups - 1, shard, cols), BF16),
            pltpu.VMEM((head_groups - 1, shard, cols), BF16),
            pltpu.VMEM((head_groups - 1, shard, cols), BF16),
            pltpu.VMEM((shard, 2 * heads * width), BF16),
            pltpu.VMEM((back + 1, stat_rows, shard), F32),
            pltpu.VMEM((lines, stat_rows, shard), F32),
            pltpu.SemaphoreType.DMA((5,)),
            pltpu.SemaphoreType.DMA((copies,)),
            pltpu.SemaphoreType.DMA((copies,)),
        ],
        compiler_params=pltpu.CompilerParams(
            collective_id=0, has_side_effects=True, vmem_limit_bytes=52 * 1024 * 1024
        ),
    )(
        jnp.swapaxes(qkv, 2, 3),
        out_weight.reshape(2 * heads * width, model),
        out_grad,
    )
    return mixed, jnp.swapaxes(grads, 2, 3)


def solution(mesh):
    return jax.shard_map(
        functools.partial(shards, mesh.shape["seq"], mesh.shape["head"]),
        mesh=mesh,
        in_specs=(
            P(None, None, "seq", "head", None),
            P(None, "head", None, None),
            P("seq", "head"),
        ),
        out_specs=(P("seq", "head"), P(None, None, "seq", "head", None)),
        check_vma=False,
    )
```

```python
import functools
import math

import jax
import jax.numpy as jnp
from jax import lax
from jax.experimental import pallas as pl
from jax.experimental.pallas import tpu as pltpu
from jax.sharding import PartitionSpec as P

ROW = 512
MESH = pl.DeviceIdType.MESH
F32 = jnp.float32
BF16 = jnp.bfloat16


def dot_nn(a, b):
    return lax.dot_general(a, b, (((1,), (0,)), ((), ())), preferred_element_type=F32)


def dot_nt(a, b):
    return lax.dot_general(a, b, (((1,), (1,)), ((), ())), preferred_element_type=F32)


def layer_kernel(
    seq_count, head_groups, back, lines, spans,
    qkv_hbm, w_hbm, og_hbm, mixed, grads,
    w, qkv, og, kvw, qw, dow, skv, sqw, sdow, ogf, mxs, mxr, att, near_stats, far_stats, in_sem, ss, rs,
):
    r = lax.axis_index("seq")
    me = lax.axis_index("head")
    heads, shard, width = qkv.shape[2:]
    cols = og.shape[1]
    scale = 1.0 / math.sqrt(width)
    side = lax.rem(r, 2)
    mate = r + 1 - 2 * side
    far = list(range(1, lines))
    steps = list(range(2, back + 1, 2))

    def slot(d):
        return pl.ds(d * shard, shard)

    loads = [
        pltpu.make_async_copy(source, target, in_sem.at[i])
        for i, (source, target) in enumerate([
            (qkv_hbm.at[0, 1:3], kvw.at[:, :, slot(0)]),
            (qkv_hbm.at[0, 0], qw.at[:, slot(0)]),
            (og_hbm, og),
            (qkv_hbm, qkv),
            (w_hbm, w),
        ])
    ]
    for load in loads:
        load.start()

    turn = 1 - 2 * lax.rem(me, 2)
    partners = []
    for m in range(2, head_groups, 2):
        to, source = lax.rem(me + m, head_groups), lax.rem(me + head_groups - m, head_groups)
        partners += [(to, source), (to + turn, source + turn)]
    partners.append((me + turn, me + turn))

    barrier = pltpu.get_barrier_semaphore()
    expected = jnp.int32(head_groups - 1)
    for d in spans:
        for target in (r + d, r - d):
            there = (target >= 0) & (target < seq_count)
            expected = expected + jnp.where(there, 1, 0)

            @pl.when(there)
            def _(target=target):
                pl.semaphore_signal(barrier, inc=1, device_id={"seq": target}, device_id_type=MESH)
    for to, _ in partners:
        pl.semaphore_signal(barrier, inc=1, device_id={"head": to}, device_id_type=MESH)

    def after(d):
        return r + d < seq_count

    def before(d):
        return r - d >= 0

    def absent(there, *refs):
        @pl.when(jnp.logical_not(there))
        def _():
            for ref in refs:
                ref[...] = jnp.zeros(ref.shape, ref.dtype)

    for d in range(1, back + 1):
        absent(before(d), kvw.at[:, :, slot(d)])
        absent(after(d), qw.at[:, slot(d)], dow.at[:, slot(d)], near_stats.at[d])
    for j in far:
        absent(before(back * j), skv.at[j - 1])
        absent(after(back * j), sqw.at[j - 1], sdow.at[j - 1], far_stats.at[j])

    base = [0]

    def numbered(count):
        first = base[0]
        base[0] += count
        return first

    def remote(source, target, at, device):
        return pltpu.make_async_remote_copy(
            src_ref=source, dst_ref=target, send_sem=ss.at[at], recv_sem=rs.at[at],
            device_id=device, device_id_type=MESH,
        )

    class Cascade:
        def __init__(self, way, part):
            self.way, self.part = way, part
            self.rank = r if way == 1 else seq_count - 1 - r
            self.side = side if way == 1 else 1 - side
            self.at = numbered((back + 1) * heads)

        def has(self, d):
            return self.rank - d >= 0

        def onward(self, d, h):
            return remote(
                self.part(h, slot(d - 2)), self.part(h, slot(d)), self.at + d * heads + h,
                {"seq": r + 2 * self.way},
            )

        def across(self, d, h):
            source = pl.ds(pl.multiple_of((d - 1 + 2 * self.side) * shard, shard), shard)
            return remote(
                self.part(h, source), self.part(h, slot(d)), self.at + d * heads + h, {"seq": mate}
            )

        def goes_on(self, e):
            return (self.rank + 2 < seq_count) & self.has(e)

        def pass_on(self, e):
            for h in range(heads):
                if e:
                    pl.when(self.has(e))(lambda: self.onward(e, h).wait_recv())
                if e < back:
                    pl.when(self.goes_on(e))(lambda: self.onward(e + 2, h).start())
                    pl.when((self.side == 0) & self.has(e))(lambda: self.across(e + 1, h).start())
                if e:
                    pl.when((self.side == 1) & self.has(e))(lambda: self.across(e - 1, h).start())

        def finish(self, h):
            for d in range(1, back, 2):
                pl.when(self.has(d))(lambda: self.across(d, h).wait_recv())

        def sent(self):
            for h in range(heads):
                for e in [0] + steps[:-1]:
                    pl.when(self.goes_on(e))(lambda: self.onward(e + 2, h).wait_send())
                for d in range(1, back, 2):
                    pl.when(self.has(d - 1 + 2 * self.side))(lambda: self.across(d, h).wait_send())

    kv = Cascade(1, lambda h, rows: kvw.at[:, h, rows])
    query = Cascade(-1, lambda h, rows: qw.at[h, rows])
    cotangent = Cascade(-1, lambda h, rows: dow.at[h, rows])
    og_at, mx_at = numbered(head_groups), numbered(head_groups)
    skv_at, sq_at, sdo_at = numbered(lines), numbered(lines), numbered(lines)
    near_at, far_at = numbered(back + 1), numbered(lines)

    last = len(partners) - 1

    def group_of(i):
        return {"head": partners[last if i % 2 else i][0]}

    def og_copy(i):
        return remote(ogf.at[i - 1] if i % 2 else og, ogf.at[i], og_at + i, group_of(i))

    def mx_copy(i):
        return remote(mxs.at[i], mxr.at[i], mx_at + i, group_of(i))

    def skv_copy(j):
        return remote(qkv.at[1, 1:3], skv.at[j - 1], skv_at + j, {"seq": r + back * j})

    def sq_copy(j):
        return remote(qkv.at[1, 0], sqw.at[j - 1], sq_at + j, {"seq": r - back * j})

    def sdo_copy(j):
        return remote(sdow.at[lines - 1], sdow.at[j - 1], sdo_at + j, {"seq": r - back * j})

    def near_copy(d):
        return remote(near_stats.at[0], near_stats.at[d], near_at + d, {"seq": r - d})

    def far_copy(j):
        return remote(far_stats.at[0], far_stats.at[j], far_at + j, {"seq": r - back * j})

    def as_rows(columns):
        lane = lax.broadcasted_iota(jnp.int32, (shard, 128), 1)
        table = jnp.zeros((shard, 128), F32)
        for i, column in enumerate(columns):
            table = jnp.where(lane == i, column, table)
        return table.T[:near_stats.shape[1]]

    def delta_of(do, out):
        return jnp.sum(do.astype(F32) * out.astype(F32), axis=1, keepdims=True)

    for load in loads[:3]:
        load.wait()
    pl.semaphore_wait(barrier, expected)
    kv.pass_on(0)
    for i in range(0, last + 1, 2):
        og_copy(i).start()
    query.pass_on(0)
    for load in loads[3:]:
        load.wait()

    def w_cols(group):
        return w[:, pl.ds(pl.multiple_of(group * cols, cols), cols)]

    for e in steps:
        kv.pass_on(e)
        query.pass_on(e)
        if e == steps[0]:
            for i in range(0, last, 2):
                og_copy(i).wait_recv()
                og_copy(i + 1).start()
            og_copy(last).wait_recv()
            total = dot_nt(og[...], w_cols(me))
            for i in range(0, last + 1, 2):
                total += dot_nt(ogf[i], w_cols(partners[i][1]))
    for j in far:
        pl.when(after(back * j))(lambda j=j: skv_copy(j).start())
        pl.when(before(back * j))(lambda j=j: sq_copy(j).start())

    for i in range(1, last, 2):
        og_copy(i).wait_recv()
        total += dot_nt(ogf[i], w_cols(partners[i][1]))
    total = total.astype(BF16)
    for h in range(heads):
        dow[h, slot(0)] = total[:, h * width:(h + 1) * width]
        sdow[lines - 1, h] = total[:, (heads + h) * width:(heads + h + 1) * width]
    cotangent.pass_on(0)
    for j in far:
        pl.when(before(back * j))(lambda j=j: sdo_copy(j).start())

    window = (back + 1) * shard
    row = lax.broadcasted_iota(jnp.int32, (shard, window), 0)
    col = lax.broadcasted_iota(jnp.int32, (shard, window), 1)
    near = col // shard
    apart = near * shard + row - (col - near * shard)
    allowed = (apart >= 0) & (apart < ROW) & (near <= r)
    local_probs, lses, deltas = [], [], []
    for h in range(heads):
        kv.finish(h)
        q, keys, values = qw[h, slot(0)], kvw[0, h], kvw[1, h]
        scores = jnp.where(allowed, dot_nt(q, keys) * scale, -jnp.inf)
        largest = jnp.max(scores, axis=1, keepdims=True)
        raised = jnp.exp(scores - largest)
        sums = jnp.sum(raised, axis=1, keepdims=True)
        probs = raised / sums
        out = dot_nn(probs.astype(BF16), values).astype(BF16)
        att[:, h * width:(h + 1) * width] = out
        lses.append(largest + jnp.log(sums))
        deltas.append(delta_of(dow[h, slot(0)], out))
        local_probs.append(probs)
        if h == 0:
            for e in steps[:-1]:
                cotangent.pass_on(e)
    near_stats[0] = as_rows(lses + deltas)
    for d in range(1, back + 1):
        pl.when(before(d))(lambda d=d: near_copy(d).start())

    for j in far:
        pl.when(before(back * j))(lambda j=j: skv_copy(j).wait_recv())

    def key_of(j, h):
        return (qkv[1, 1, h] if j == 0 else skv[j - 1, 0, h]).astype(F32)

    def value_of(j, h):
        return (qkv[1, 2, h] if j == 0 else skv[j - 1, 1, h]).astype(F32)

    strided_probs, strided_lses, strided_deltas = [], [], []
    for h in range(heads):
        q = qkv[1, 0, h].astype(F32)
        scores = [jnp.sum(q * key_of(0, h), axis=1, keepdims=True) * scale]
        for j in far:
            score = jnp.sum(q * key_of(j, h), axis=1, keepdims=True) * scale
            scores.append(jnp.where(before(back * j), score, -jnp.inf))
        largest = functools.reduce(jnp.maximum, scores)
        raised = [jnp.exp(s - largest) for s in scores]
        sums = sum(raised)
        probs = [e / sums for e in raised]
        strided_probs.append(probs)
        out = sum(p.astype(BF16).astype(F32) * value_of(j, h) for j, p in enumerate(probs))
        out = out.astype(BF16)
        att[:, (heads + h) * width:(heads + h + 1) * width] = out
        strided_lses.append(largest + jnp.log(sums))
        strided_deltas.append(delta_of(sdow[lines - 1, h], out))
    far_stats[0] = as_rows(strided_lses + strided_deltas)
    for j in far:
        pl.when(before(back * j))(lambda j=j: far_copy(j).start())

    for i in range(1, last, 2):
        mxs[i] = dot_nn(att[...], w_cols(partners[i][0])).astype(BF16)
        mx_copy(i).start()
    for i in range(0, last, 2):
        total = dot_nn(att[...], w_cols(partners[i][0]))
        mx_copy(i + 1).wait_recv()
        mxs[i] = (total + mxr[i + 1].astype(F32)).astype(BF16)
        mx_copy(i).start()
    mxs[last] = dot_nn(att[...], w_cols(partners[last][0])).astype(BF16)
    mx_copy(last).start()
    cotangent.pass_on(back)

    for h in range(heads):
        grad_p = dot_nt(dow[h, slot(0)], kvw[1, h])
        grad_s = (local_probs[h] * (grad_p - deltas[h])).astype(BF16)
        grads[0, 0, h] = (dot_nn(grad_s, kvw[0, h]) * scale).astype(BF16)
    total = dot_nn(att[...], w_cols(me))

    strided = []
    for h in range(heads):
        q, do = qkv[1, 0, h].astype(F32), sdow[lines - 1, h].astype(F32)
        delta = strided_deltas[h]
        grad_q = jnp.zeros_like(q)
        for j in [0] + far:
            prob = strided_probs[h][j]
            grad_p = jnp.sum(do * value_of(j, h), axis=1, keepdims=True)
            grad_s = (prob * (grad_p - delta)).astype(BF16).astype(F32)
            grad_q += grad_s * key_of(j, h)
            if j == 0:
                strided.append((grad_s * q, prob.astype(BF16).astype(F32) * do))
        grads[1, 0, h] = (grad_q * scale).astype(BF16)

    for d in range(1, back + 1):
        pl.when(after(d))(lambda d=d: near_copy(d).wait_recv())
    apart = col - row
    allowed = (apart >= 0) & (apart < ROW) & (near < seq_count - r)
    for h in range(heads):
        query.finish(h)
        cotangent.finish(h)
        queries, dos, key, value = qw[h], dow[h], kvw[0, h, slot(0)], kvw[1, h, slot(0)]
        lse = jnp.concatenate([near_stats[d, h:h + 1] for d in range(back + 1)], axis=1)
        rows = [near_stats[d, heads + h:heads + h + 1] for d in range(back + 1)]
        delta = jnp.concatenate(rows, axis=1)
        probs = jnp.exp(jnp.where(allowed, dot_nt(key, queries) * scale - lse, -jnp.inf))
        grad_s = (probs * (dot_nt(value, dos) - delta)).astype(BF16)
        grads[0, 1, h] = (dot_nn(grad_s, queries) * scale).astype(BF16)
        grads[0, 2, h] = dot_nn(probs.astype(BF16), dos).astype(BF16)

    for j in far:
        @pl.when(after(back * j))
        def _(j=j):
            sq_copy(j).wait_recv()
            sdo_copy(j).wait_recv()
            far_copy(j).wait_recv()
    for j in far:
        rows = far_stats[j]
        table = jnp.concatenate([rows] * (128 // rows.shape[0]), axis=0).T
        for h in range(heads):
            q, do = sqw[j - 1, h].astype(F32), sdow[j - 1, h].astype(F32)
            lse = table[:, h:h + 1]
            delta = table[:, heads + h:heads + h + 1]
            score = jnp.sum(q * key_of(0, h), axis=1, keepdims=True) * scale
            prob = jnp.exp(jnp.where(after(back * j), score - lse, -jnp.inf))
            grad_p = jnp.sum(do * value_of(0, h), axis=1, keepdims=True)
            grad_s = (prob * (grad_p - delta)).astype(BF16).astype(F32)
            grad_k, grad_v = strided[h]
            strided[h] = (grad_k + grad_s * q, grad_v + prob.astype(BF16).astype(F32) * do)
    for h in range(heads):
        grads[1, 1, h] = (strided[h][0] * scale).astype(BF16)
        grads[1, 2, h] = strided[h][1].astype(BF16)

    for i in range(last, -1, -2):
        mx_copy(i).wait_recv()
        total += mxr[i].astype(F32)
    mixed[...] = total.astype(BF16)

    for i in range(len(partners)):
        og_copy(i).wait_send()
        mx_copy(i).wait_send()
    for cascade in (kv, query, cotangent):
        cascade.sent()
    for j in far:
        pl.when(after(back * j))(lambda j=j: skv_copy(j).wait_send())

        @pl.when(before(back * j))
        def _(j=j):
            sq_copy(j).wait_send()
            sdo_copy(j).wait_send()
            far_copy(j).wait_send()
    for d in range(1, back + 1):
        pl.when(before(d))(lambda d=d: near_copy(d).wait_send())


def shards(seq_count, head_groups, qkv, out_weight, out_grad):
    _, _, shard, heads, width = qkv.shape
    back = ROW // shard
    assert back * shard == ROW and back % 2 == 0 and seq_count % back == 0
    assert head_groups % 2 == 0
    lines = seq_count // back
    others = max(1, lines - 1)
    spans = list(range(1, back + 1))
    spans += [back * j for j in range(2, lines)]
    model = out_weight.shape[-1]
    cols = out_grad.shape[1]
    window = (back + 1) * shard
    stat_rows = 2 * heads
    while 128 % stat_rows or stat_rows % 8:
        stat_rows += 1
    copies = 2 * head_groups + 3 * lines + 3 * (back + 1) * heads + back + 1 + lines
    vmem = pl.BlockSpec(memory_space=pltpu.VMEM)
    hbm = pl.BlockSpec(memory_space=pltpu.HBM)
    mixed, grads = pl.pallas_call(
        functools.partial(layer_kernel, seq_count, head_groups, back, lines, spans),
        out_shape=[
            jax.ShapeDtypeStruct((shard, cols), BF16),
            jax.ShapeDtypeStruct((2, 3, heads, shard, width), BF16),
        ],
        in_specs=[pl.BlockSpec(memory_space=pl.ANY), hbm, hbm],
        out_specs=[vmem, vmem],
        scratch_shapes=[
            pltpu.VMEM((2 * heads * width, model), BF16),
            pltpu.VMEM((2, 3, heads, shard, width), BF16),
            pltpu.VMEM((shard, cols), BF16),
            pltpu.VMEM((2, heads, window, width), BF16),
            pltpu.VMEM((heads, window, width), BF16),
            pltpu.VMEM((heads, window, width), BF16),
            pltpu.VMEM((others, 2, heads, shard, width), BF16),
            pltpu.VMEM((others, heads, shard, width), BF16),
            pltpu.VMEM((lines, heads, shard, width), BF16),
            pltpu.VMEM((head_groups - 1, shard, cols), BF16),
            pltpu.VMEM((head_groups - 1, shard, cols), BF16),
            pltpu.VMEM((head_groups - 1, shard, cols), BF16),
            pltpu.VMEM((shard, 2 * heads * width), BF16),
            pltpu.VMEM((back + 1, stat_rows, shard), F32),
            pltpu.VMEM((lines, stat_rows, shard), F32),
            pltpu.SemaphoreType.DMA((5,)),
            pltpu.SemaphoreType.DMA((copies,)),
            pltpu.SemaphoreType.DMA((copies,)),
        ],
        compiler_params=pltpu.CompilerParams(
            collective_id=0, has_side_effects=True, vmem_limit_bytes=52 * 1024 * 1024
        ),
    )(
        jnp.swapaxes(qkv, 2, 3),
        out_weight.reshape(2 * heads * width, model),
        out_grad,
    )
    return mixed, jnp.swapaxes(grads, 2, 3)


def solution(mesh):
    return jax.shard_map(
        functools.partial(shards, mesh.shape["seq"], mesh.shape["head"]),
        mesh=mesh,
        in_specs=(
            P(None, None, "seq", "head", None),
            P(None, "head", None, None),
            P("seq", "head"),
        ),
        out_specs=(P("seq", "head"), P(None, None, "seq", "head", None)),
        check_vma=False,
    )
```

```python
import functools
import math

import jax
import jax.numpy as jnp
from jax import lax
from jax.experimental import pallas as pl
from jax.experimental.pallas import tpu as pltpu
from jax.sharding import PartitionSpec as P

ROW = 512
MESH = pl.DeviceIdType.MESH
F32 = jnp.float32
BF16 = jnp.bfloat16


def dot_nn(a, b):
    return lax.dot_general(a, b, (((1,), (0,)), ((), ())), preferred_element_type=F32)


def dot_nt(a, b):
    return lax.dot_general(a, b, (((1,), (1,)), ((), ())), preferred_element_type=F32)


def layer_kernel(
    seq_count, head_groups, back, lines, spans,
    qkv_hbm, w_hbm, og_hbm, mixed, grads,
    w, qkv, og, kvw, qw, dow, skv, sqw, sdow, ogf, mxs, mxr, att, near_stats, far_stats, in_sem, ss, rs,
):
    r = lax.axis_index("seq")
    me = lax.axis_index("head")
    heads, shard, width = qkv.shape[2:]
    cols = og.shape[1]
    scale = 1.0 / math.sqrt(width)
    side = lax.rem(r, 2)
    mate = r + 1 - 2 * side
    far = list(range(1, lines))
    steps = list(range(2, back + 1, 2))

    def slot(d):
        return pl.ds(d * shard, shard)

    loads = [
        pltpu.make_async_copy(source, target, in_sem.at[i])
        for i, (source, target) in enumerate([
            (qkv_hbm.at[0, 1:3], kvw.at[:, :, slot(0)]),
            (qkv_hbm.at[0, 0], qw.at[:, slot(0)]),
            (og_hbm, og),
            (qkv_hbm, qkv),
            (w_hbm, w),
        ])
    ]
    for load in loads:
        load.start()

    turn = 1 - 2 * lax.rem(me, 2)
    partners = []
    for m in range(2, head_groups, 2):
        to, source = lax.rem(me + m, head_groups), lax.rem(me + head_groups - m, head_groups)
        partners += [(to, source), (to + turn, source + turn)]
    partners.append((me + turn, me + turn))

    barrier = pltpu.get_barrier_semaphore()
    expected = jnp.int32(head_groups - 1)
    for d in spans:
        for target in (r + d, r - d):
            there = (target >= 0) & (target < seq_count)
            expected = expected + jnp.where(there, 1, 0)

            @pl.when(there)
            def _(target=target):
                pl.semaphore_signal(barrier, inc=1, device_id={"seq": target}, device_id_type=MESH)
    for to, _ in partners:
        pl.semaphore_signal(barrier, inc=1, device_id={"head": to}, device_id_type=MESH)

    def after(d):
        return r + d < seq_count

    def before(d):
        return r - d >= 0

    def absent(there, *refs):
        @pl.when(jnp.logical_not(there))
        def _():
            for ref in refs:
                ref[...] = jnp.zeros(ref.shape, ref.dtype)

    for d in range(1, back + 1):
        absent(before(d), kvw.at[:, :, slot(d)])
        absent(after(d), qw.at[:, slot(d)], dow.at[:, slot(d)], near_stats.at[d])
    for j in far:
        absent(before(back * j), skv.at[j - 1])
        absent(after(back * j), sqw.at[j - 1], sdow.at[j - 1], far_stats.at[j])

    base = [0]

    def numbered(count):
        first = base[0]
        base[0] += count
        return first

    def remote(source, target, at, device):
        return pltpu.make_async_remote_copy(
            src_ref=source, dst_ref=target, send_sem=ss.at[at], recv_sem=rs.at[at],
            device_id=device, device_id_type=MESH,
        )

    class Cascade:
        def __init__(self, way, part):
            self.way, self.part = way, part
            self.rank = r if way == 1 else seq_count - 1 - r
            self.side = side if way == 1 else 1 - side
            self.at = numbered((back + 1) * heads)

        def has(self, d):
            return self.rank - d >= 0

        def onward(self, d, h):
            return remote(
                self.part(h, slot(d - 2)), self.part(h, slot(d)), self.at + d * heads + h,
                {"seq": r + 2 * self.way},
            )

        def across(self, d, h):
            source = pl.ds(pl.multiple_of((d - 1 + 2 * self.side) * shard, shard), shard)
            return remote(
                self.part(h, source), self.part(h, slot(d)), self.at + d * heads + h, {"seq": mate}
            )

        def goes_on(self, e):
            return (self.rank + 2 < seq_count) & self.has(e)

        def pass_on(self, e):
            for h in range(heads):
                if e:
                    pl.when(self.has(e))(lambda: self.onward(e, h).wait_recv())
                if e < back:
                    pl.when(self.goes_on(e))(lambda: self.onward(e + 2, h).start())
                    pl.when((self.side == 0) & self.has(e))(lambda: self.across(e + 1, h).start())
                if e:
                    pl.when((self.side == 1) & self.has(e))(lambda: self.across(e - 1, h).start())

        def finish(self, h):
            for d in range(1, back, 2):
                pl.when(self.has(d))(lambda: self.across(d, h).wait_recv())

        def sent(self):
            for h in range(heads):
                for e in [0] + steps[:-1]:
                    pl.when(self.goes_on(e))(lambda: self.onward(e + 2, h).wait_send())
                for d in range(1, back, 2):
                    pl.when(self.has(d - 1 + 2 * self.side))(lambda: self.across(d, h).wait_send())

    kv = Cascade(1, lambda h, rows: kvw.at[:, h, rows])
    query = Cascade(-1, lambda h, rows: qw.at[h, rows])
    cotangent = Cascade(-1, lambda h, rows: dow.at[h, rows])
    og_at, mx_at = numbered(head_groups), numbered(head_groups)
    skv_at, sq_at, sdo_at = numbered(lines), numbered(lines), numbered(lines)
    near_at, far_at = numbered((back + 1) * heads), numbered(lines)

    def og_copy(i):
        return remote(og, ogf.at[i], og_at + i, {"head": partners[i][0]})

    def mx_copy(i):
        return remote(mxs.at[i], mxr.at[i], mx_at + i, {"head": partners[i][0]})

    def skv_copy(j):
        return remote(qkv.at[1, 1:3], skv.at[j - 1], skv_at + j, {"seq": r + back * j})

    def sq_copy(j):
        return remote(qkv.at[1, 0], sqw.at[j - 1], sq_at + j, {"seq": r - back * j})

    def sdo_copy(j):
        return remote(sdow.at[lines - 1], sdow.at[j - 1], sdo_at + j, {"seq": r - back * j})

    def near_copy(d, h):
        at = near_at + d * heads + h
        return remote(near_stats.at[0, h], near_stats.at[d, h], at, {"seq": r - d})

    def far_copy(j):
        return remote(far_stats.at[0], far_stats.at[j], far_at + j, {"seq": r - back * j})

    def as_rows(columns):
        lane = lax.broadcasted_iota(jnp.int32, (shard, 128), 1)
        table = jnp.zeros((shard, 128), F32)
        for i, column in enumerate(columns):
            table = jnp.where(lane == i, column, table)
        return table.T[:far_stats.shape[1]]

    def delta_of(do, out):
        return jnp.sum(do.astype(F32) * out.astype(F32), axis=1, keepdims=True)

    for load in loads[:3]:
        load.wait()
    pl.semaphore_wait(barrier, expected)
    kv.pass_on(0)
    for i in range(len(partners)):
        og_copy(i).start()
    query.pass_on(0)
    for load in loads[3:]:
        load.wait()

    def w_cols(group):
        return w[:, pl.ds(pl.multiple_of(group * cols, cols), cols)]

    total = dot_nt(og[...], w_cols(me))
    for e in steps:
        kv.pass_on(e)
        query.pass_on(e)
    for j in far:
        pl.when(after(back * j))(lambda j=j: skv_copy(j).start())
        pl.when(before(back * j))(lambda j=j: sq_copy(j).start())

    for i in reversed(range(len(partners))):
        og_copy(i).wait_recv()
        total += dot_nt(ogf[i], w_cols(partners[i][1]))
    total = total.astype(BF16)
    for h in range(heads):
        dow[h, slot(0)] = total[:, h * width:(h + 1) * width]
        sdow[lines - 1, h] = total[:, (heads + h) * width:(heads + h + 1) * width]
    cotangent.pass_on(0)

    window = (back + 1) * shard
    row = lax.broadcasted_iota(jnp.int32, (shard, window), 0)
    col = lax.broadcasted_iota(jnp.int32, (shard, window), 1)
    near = col // shard
    apart = near * shard + row - (col - near * shard)
    allowed = (apart >= 0) & (apart < ROW) & (near <= r)
    local_probs, deltas = [], []
    for h in range(heads):
        kv.finish(h)
        q, keys, values = qw[h, slot(0)], kvw[0, h], kvw[1, h]
        scores = jnp.where(allowed, dot_nt(q, keys) * scale, -jnp.inf)
        largest = jnp.max(scores, axis=1, keepdims=True)
        raised = jnp.exp(scores - largest)
        sums = jnp.sum(raised, axis=1, keepdims=True)
        probs = raised / sums
        out = dot_nn(probs.astype(BF16), values).astype(BF16)
        att[:, h * width:(h + 1) * width] = out
        deltas.append(delta_of(dow[h, slot(0)], out))
        local_probs.append(probs)
        near_stats[0, h] = as_rows([largest + jnp.log(sums), deltas[h]])
        for d in range(1, back + 1):
            pl.when(before(d))(lambda d=d, h=h: near_copy(d, h).start())
        if h == 0:
            for e in steps[:-1]:
                cotangent.pass_on(e)
            for j in far:
                pl.when(before(back * j))(lambda j=j: sdo_copy(j).start())

    for j in far:
        pl.when(before(back * j))(lambda j=j: skv_copy(j).wait_recv())

    def key_of(j, h):
        return (qkv[1, 1, h] if j == 0 else skv[j - 1, 0, h]).astype(F32)

    def value_of(j, h):
        return (qkv[1, 2, h] if j == 0 else skv[j - 1, 1, h]).astype(F32)

    strided_probs, strided_lses, strided_deltas = [], [], []
    for h in range(heads):
        q = qkv[1, 0, h].astype(F32)
        scores = [jnp.sum(q * key_of(0, h), axis=1, keepdims=True) * scale]
        for j in far:
            score = jnp.sum(q * key_of(j, h), axis=1, keepdims=True) * scale
            scores.append(jnp.where(before(back * j), score, -jnp.inf))
        largest = functools.reduce(jnp.maximum, scores)
        raised = [jnp.exp(s - largest) for s in scores]
        sums = sum(raised)
        probs = [e / sums for e in raised]
        strided_probs.append(probs)
        out = sum(p.astype(BF16).astype(F32) * value_of(j, h) for j, p in enumerate(probs))
        out = out.astype(BF16)
        att[:, (heads + h) * width:(heads + h + 1) * width] = out
        strided_lses.append(largest + jnp.log(sums))
        strided_deltas.append(delta_of(sdow[lines - 1, h], out))
    far_stats[0] = as_rows(strided_lses + strided_deltas)
    for j in far:
        pl.when(before(back * j))(lambda j=j: far_copy(j).start())

    for i, (to, _) in enumerate(partners):
        mxs[i] = dot_nn(att[...], w_cols(to)).astype(BF16)
        mx_copy(i).start()
    cotangent.pass_on(back)

    for h in range(heads):
        grad_p = dot_nt(dow[h, slot(0)], kvw[1, h])
        grad_s = (local_probs[h] * (grad_p - deltas[h])).astype(BF16)
        grads[0, 0, h] = (dot_nn(grad_s, kvw[0, h]) * scale).astype(BF16)
    total = dot_nn(att[...], w_cols(me))

    strided = []
    for h in range(heads):
        q, do = qkv[1, 0, h].astype(F32), sdow[lines - 1, h].astype(F32)
        delta = strided_deltas[h]
        grad_q = jnp.zeros_like(q)
        for j in [0] + far:
            prob = strided_probs[h][j]
            grad_p = jnp.sum(do * value_of(j, h), axis=1, keepdims=True)
            grad_s = (prob * (grad_p - delta)).astype(BF16).astype(F32)
            grad_q += grad_s * key_of(j, h)
            if j == 0:
                strided.append((grad_s * q, prob.astype(BF16).astype(F32) * do))
        grads[1, 0, h] = (grad_q * scale).astype(BF16)

    apart = col - row
    allowed = (apart >= 0) & (apart < ROW) & (near < seq_count - r)
    for h in range(heads):
        query.finish(h)
        cotangent.finish(h)
        for d in range(1, back + 1):
            pl.when(after(d))(lambda d=d, h=h: near_copy(d, h).wait_recv())
        queries, dos, key, value = qw[h], dow[h], kvw[0, h, slot(0)], kvw[1, h, slot(0)]
        lse = jnp.concatenate([near_stats[d, h, 0:1] for d in range(back + 1)], axis=1)
        rows = [near_stats[d, h, 1:2] for d in range(back + 1)]
        delta = jnp.concatenate(rows, axis=1)
        probs = jnp.exp(jnp.where(allowed, dot_nt(key, queries) * scale - lse, -jnp.inf))
        grad_s = (probs * (dot_nt(value, dos) - delta)).astype(BF16)
        grads[0, 1, h] = (dot_nn(grad_s, queries) * scale).astype(BF16)
        grads[0, 2, h] = dot_nn(probs.astype(BF16), dos).astype(BF16)

    for j in far:
        @pl.when(after(back * j))
        def _(j=j):
            sq_copy(j).wait_recv()
            sdo_copy(j).wait_recv()
            far_copy(j).wait_recv()
    for j in far:
        rows = far_stats[j]
        table = jnp.concatenate([rows] * (128 // rows.shape[0]), axis=0).T
        for h in range(heads):
            q, do = sqw[j - 1, h].astype(F32), sdow[j - 1, h].astype(F32)
            lse = table[:, h:h + 1]
            delta = table[:, heads + h:heads + h + 1]
            score = jnp.sum(q * key_of(0, h), axis=1, keepdims=True) * scale
            prob = jnp.exp(jnp.where(after(back * j), score - lse, -jnp.inf))
            grad_p = jnp.sum(do * value_of(0, h), axis=1, keepdims=True)
            grad_s = (prob * (grad_p - delta)).astype(BF16).astype(F32)
            grad_k, grad_v = strided[h]
            strided[h] = (grad_k + grad_s * q, grad_v + prob.astype(BF16).astype(F32) * do)
    for h in range(heads):
        grads[1, 1, h] = (strided[h][0] * scale).astype(BF16)
        grads[1, 2, h] = strided[h][1].astype(BF16)

    for i in reversed(range(len(partners))):
        mx_copy(i).wait_recv()
        total += mxr[i].astype(F32)
    mixed[...] = total.astype(BF16)

    for i in range(len(partners)):
        og_copy(i).wait_send()
        mx_copy(i).wait_send()
    for cascade in (kv, query, cotangent):
        cascade.sent()
    for j in far:
        pl.when(after(back * j))(lambda j=j: skv_copy(j).wait_send())

        @pl.when(before(back * j))
        def _(j=j):
            sq_copy(j).wait_send()
            sdo_copy(j).wait_send()
            far_copy(j).wait_send()
    for d in range(1, back + 1):
        for h in range(heads):
            pl.when(before(d))(lambda d=d, h=h: near_copy(d, h).wait_send())


def shards(seq_count, head_groups, qkv, out_weight, out_grad):
    _, _, shard, heads, width = qkv.shape
    back = ROW // shard
    assert back * shard == ROW and back % 2 == 0 and seq_count % back == 0
    assert head_groups % 2 == 0
    lines = seq_count // back
    others = max(1, lines - 1)
    spans = list(range(1, back + 1))
    spans += [back * j for j in range(2, lines)]
    model = out_weight.shape[-1]
    cols = out_grad.shape[1]
    window = (back + 1) * shard
    stat_rows = 2 * heads
    while 128 % stat_rows or stat_rows % 8:
        stat_rows += 1
    copies = 2 * head_groups + 3 * lines + 4 * (back + 1) * heads + lines
    vmem = pl.BlockSpec(memory_space=pltpu.VMEM)
    hbm = pl.BlockSpec(memory_space=pltpu.HBM)
    mixed, grads = pl.pallas_call(
        functools.partial(layer_kernel, seq_count, head_groups, back, lines, spans),
        out_shape=[
            jax.ShapeDtypeStruct((shard, cols), BF16),
            jax.ShapeDtypeStruct((2, 3, heads, shard, width), BF16),
        ],
        in_specs=[pl.BlockSpec(memory_space=pl.ANY), hbm, hbm],
        out_specs=[vmem, vmem],
        scratch_shapes=[
            pltpu.VMEM((2 * heads * width, model), BF16),
            pltpu.VMEM((2, 3, heads, shard, width), BF16),
            pltpu.VMEM((shard, cols), BF16),
            pltpu.VMEM((2, heads, window, width), BF16),
            pltpu.VMEM((heads, window, width), BF16),
            pltpu.VMEM((heads, window, width), BF16),
            pltpu.VMEM((others, 2, heads, shard, width), BF16),
            pltpu.VMEM((others, heads, shard, width), BF16),
            pltpu.VMEM((lines, heads, shard, width), BF16),
            pltpu.VMEM((head_groups - 1, shard, cols), BF16),
            pltpu.VMEM((head_groups - 1, shard, cols), BF16),
            pltpu.VMEM((head_groups - 1, shard, cols), BF16),
            pltpu.VMEM((shard, 2 * heads * width), BF16),
            pltpu.VMEM((back + 1, heads, stat_rows, shard), F32),
            pltpu.VMEM((lines, stat_rows, shard), F32),
            pltpu.SemaphoreType.DMA((5,)),
            pltpu.SemaphoreType.DMA((copies,)),
            pltpu.SemaphoreType.DMA((copies,)),
        ],
        compiler_params=pltpu.CompilerParams(
            collective_id=0, has_side_effects=True, vmem_limit_bytes=52 * 1024 * 1024
        ),
    )(
        jnp.swapaxes(qkv, 2, 3),
        out_weight.reshape(2 * heads * width, model),
        out_grad,
    )
    return mixed, jnp.swapaxes(grads, 2, 3)


def solution(mesh):
    return jax.shard_map(
        functools.partial(shards, mesh.shape["seq"], mesh.shape["head"]),
        mesh=mesh,
        in_specs=(
            P(None, None, "seq", "head", None),
            P(None, "head", None, None),
            P("seq", "head"),
        ),
        out_specs=(P("seq", "head"), P(None, None, "seq", "head", None)),
        check_vma=False,
    )
```

```python
import functools
import math

import jax
import jax.numpy as jnp
from jax import lax
from jax.experimental import pallas as pl
from jax.experimental.pallas import tpu as pltpu
from jax.sharding import PartitionSpec as P

ROW = 512
MESH = pl.DeviceIdType.MESH
F32 = jnp.float32
BF16 = jnp.bfloat16


def dot_nn(a, b):
    return lax.dot_general(a, b, (((1,), (0,)), ((), ())), preferred_element_type=F32)


def dot_nt(a, b):
    return lax.dot_general(a, b, (((1,), (1,)), ((), ())), preferred_element_type=F32)


def layer_kernel(
    seq_count, head_groups, back, lines, spans,
    qkv_hbm, w_hbm, og_hbm, mixed, grads,
    w, qkv, og, kvw, qw, dow, skv, sqw, sdow, ogf, mxs, mxr, att, near_stats, far_stats, in_sem, ss, rs,
):
    r = lax.axis_index("seq")
    me = lax.axis_index("head")
    heads, shard, width = qkv.shape[2:]
    cols = og.shape[1]
    scale = 1.0 / math.sqrt(width)
    side = lax.rem(r, 2)
    mate = r + 1 - 2 * side
    far = list(range(1, lines))
    steps = list(range(2, back + 1, 2))

    def slot(d):
        return pl.ds(d * shard, shard)

    loads = [
        pltpu.make_async_copy(source, target, in_sem.at[i])
        for i, (source, target) in enumerate([
            (qkv_hbm.at[0, 1:3], kvw.at[:, :, slot(0)]),
            (qkv_hbm.at[0, 0], qw.at[:, slot(0)]),
            (og_hbm, og),
            (qkv_hbm, qkv),
            (w_hbm, w),
        ])
    ]
    for load in loads:
        load.start()

    turn = 1 - 2 * lax.rem(me, 2)
    partners = []
    for m in range(2, head_groups, 2):
        to, source = lax.rem(me + m, head_groups), lax.rem(me + head_groups - m, head_groups)
        partners += [(to, source), (to + turn, source + turn)]
    partners.append((me + turn, me + turn))

    barrier = pltpu.get_barrier_semaphore()
    expected = jnp.int32(head_groups - 1)
    for d in spans:
        for target in (r + d, r - d):
            there = (target >= 0) & (target < seq_count)
            expected = expected + jnp.where(there, 1, 0)

            @pl.when(there)
            def _(target=target):
                pl.semaphore_signal(barrier, inc=1, device_id={"seq": target}, device_id_type=MESH)
    for to, _ in partners:
        pl.semaphore_signal(barrier, inc=1, device_id={"head": to}, device_id_type=MESH)

    def after(d):
        return r + d < seq_count

    def before(d):
        return r - d >= 0

    def absent(there, *refs):
        @pl.when(jnp.logical_not(there))
        def _():
            for ref in refs:
                ref[...] = jnp.zeros(ref.shape, ref.dtype)

    for d in range(1, back + 1):
        absent(before(d), kvw.at[:, :, slot(d)])
        absent(after(d), qw.at[:, slot(d)], dow.at[:, slot(d)], near_stats.at[d])
    for j in far:
        absent(before(back * j), skv.at[j - 1])
        absent(after(back * j), sqw.at[j - 1], sdow.at[j - 1], far_stats.at[j])

    base = [0]

    def numbered(count):
        first = base[0]
        base[0] += count
        return first

    def remote(source, target, at, device):
        return pltpu.make_async_remote_copy(
            src_ref=source, dst_ref=target, send_sem=ss.at[at], recv_sem=rs.at[at],
            device_id=device, device_id_type=MESH,
        )

    class Cascade:
        def __init__(self, way, part):
            self.way, self.part = way, part
            self.rank = r if way == 1 else seq_count - 1 - r
            self.side = side if way == 1 else 1 - side
            self.at = numbered((back + 1) * heads)

        def has(self, d):
            return self.rank - d >= 0

        def onward(self, d, h):
            return remote(
                self.part(h, slot(d - 2)), self.part(h, slot(d)), self.at + d * heads + h,
                {"seq": r + 2 * self.way},
            )

        def across(self, d, h):
            source = pl.ds(pl.multiple_of((d - 1 + 2 * self.side) * shard, shard), shard)
            return remote(
                self.part(h, source), self.part(h, slot(d)), self.at + d * heads + h, {"seq": mate}
            )

        def goes_on(self, e):
            return (self.rank + 2 < seq_count) & self.has(e)

        def pass_on(self, e):
            for h in range(heads):
                if e:
                    pl.when(self.has(e))(lambda: self.onward(e, h).wait_recv())
                if e < back:
                    pl.when(self.goes_on(e))(lambda: self.onward(e + 2, h).start())
                    pl.when((self.side == 0) & self.has(e))(lambda: self.across(e + 1, h).start())
                if e:
                    pl.when((self.side == 1) & self.has(e))(lambda: self.across(e - 1, h).start())

        def finish(self, h):
            for d in range(1, back, 2):
                pl.when(self.has(d))(lambda: self.across(d, h).wait_recv())

        def sent(self):
            for h in range(heads):
                for e in [0] + steps[:-1]:
                    pl.when(self.goes_on(e))(lambda: self.onward(e + 2, h).wait_send())
                for d in range(1, back, 2):
                    pl.when(self.has(d - 1 + 2 * self.side))(lambda: self.across(d, h).wait_send())

    kv = Cascade(1, lambda h, rows: kvw.at[:, h, rows])
    query = Cascade(-1, lambda h, rows: qw.at[h, rows])
    cotangent = Cascade(-1, lambda h, rows: dow.at[h, rows])
    og_at, mx_at = numbered(head_groups), numbered(head_groups)
    skv_at, sq_at, sdo_at = numbered(lines), numbered(lines), numbered(lines)
    near_at, far_at = numbered(back + 1), numbered(lines)

    def og_copy(i):
        return remote(og, ogf.at[i], og_at + i, {"head": partners[i][0]})

    def mx_copy(i):
        return remote(mxs.at[i], mxr.at[i], mx_at + i, {"head": partners[i][0]})

    def skv_copy(j):
        return remote(qkv.at[1, 1:3], skv.at[j - 1], skv_at + j, {"seq": r + back * j})

    def sq_copy(j):
        return remote(qkv.at[1, 0], sqw.at[j - 1], sq_at + j, {"seq": r - back * j})

    def sdo_copy(j):
        return remote(sdow.at[lines - 1], sdow.at[j - 1], sdo_at + j, {"seq": r - back * j})

    def near_copy(d):
        return remote(near_stats.at[0], near_stats.at[d], near_at + d, {"seq": r - d})

    def far_copy(j):
        return remote(far_stats.at[0], far_stats.at[j], far_at + j, {"seq": r - back * j})

    def as_rows(columns):
        lane = lax.broadcasted_iota(jnp.int32, (shard, 128), 1)
        table = jnp.zeros((shard, 128), F32)
        for i, column in enumerate(columns):
            table = jnp.where(lane == i, column, table)
        return table.T[:near_stats.shape[1]]

    def delta_of(do, out):
        return jnp.sum(do.astype(F32) * out.astype(F32), axis=1, keepdims=True)

    for load in loads[:3]:
        load.wait()
    pl.semaphore_wait(barrier, expected)
    kv.pass_on(0)
    for i in range(len(partners)):
        og_copy(i).start()
    query.pass_on(0)
    for load in loads[3:]:
        load.wait()

    def w_cols(group):
        return w[:, pl.ds(pl.multiple_of(group * cols, cols), cols)]

    total = dot_nt(og[...], w_cols(me))
    for e in steps:
        kv.pass_on(e)
        query.pass_on(e)
    for j in far:
        pl.when(after(back * j))(lambda j=j: skv_copy(j).start())
        pl.when(before(back * j))(lambda j=j: sq_copy(j).start())

    for i in reversed(range(len(partners))):
        og_copy(i).wait_recv()
        total += dot_nt(ogf[i], w_cols(partners[i][1]))
    total = total.astype(BF16)
    for h in range(heads):
        dow[h, slot(0)] = total[:, h * width:(h + 1) * width]
        sdow[lines - 1, h] = total[:, (heads + h) * width:(heads + h + 1) * width]
    cotangent.pass_on(0)
    for j in far:
        pl.when(before(back * j))(lambda j=j: sdo_copy(j).start())

    ahead = lax.broadcasted_iota(jnp.int32, (shard, shard), 0) - lax.broadcasted_iota(
        jnp.int32, (shard, shard), 1
    )

    def band(ahead, there):
        blocks = [d * shard + ahead for d in range(back + 1)]
        blocks = [(a >= 0) & (a < ROW) & there(d) for d, a in enumerate(blocks)]
        return jnp.concatenate(blocks, axis=1)

    allowed = band(ahead, before)
    local_probs, lses, deltas = [], [], []
    for h in range(heads):
        kv.finish(h)
        q, keys, values = qw[h, slot(0)], kvw[0, h], kvw[1, h]
        scores = jnp.where(allowed, dot_nt(q, keys) * scale, -jnp.inf)
        largest = jnp.max(scores, axis=1, keepdims=True)
        raised = jnp.exp(scores - largest)
        sums = jnp.sum(raised, axis=1, keepdims=True)
        probs = raised * (1.0 / sums)
        out = dot_nn(probs.astype(BF16), values).astype(BF16)
        att[:, h * width:(h + 1) * width] = out
        lses.append(largest + jnp.log(sums))
        deltas.append(delta_of(dow[h, slot(0)], out))
        local_probs.append(probs)
    near_stats[0] = as_rows(lses + deltas)
    for d in range(1, back + 1):
        pl.when(before(d))(lambda d=d: near_copy(d).start())
    for e in steps[:-1]:
        cotangent.pass_on(e)

    for j in far:
        pl.when(before(back * j))(lambda j=j: skv_copy(j).wait_recv())

    def key_of(j, h):
        return (qkv[1, 1, h] if j == 0 else skv[j - 1, 0, h]).astype(F32)

    def value_of(j, h):
        return (qkv[1, 2, h] if j == 0 else skv[j - 1, 1, h]).astype(F32)

    strided_probs, strided_lses, strided_deltas = [], [], []
    for h in range(heads):
        q = qkv[1, 0, h].astype(F32)
        scores = [jnp.sum(q * key_of(0, h), axis=1, keepdims=True) * scale]
        for j in far:
            score = jnp.sum(q * key_of(j, h), axis=1, keepdims=True) * scale
            scores.append(jnp.where(before(back * j), score, -jnp.inf))
        largest = functools.reduce(jnp.maximum, scores)
        raised = [jnp.exp(s - largest) for s in scores]
        sums = sum(raised)
        probs = [e / sums for e in raised]
        strided_probs.append(probs)
        out = sum(p.astype(BF16).astype(F32) * value_of(j, h) for j, p in enumerate(probs))
        out = out.astype(BF16)
        att[:, (heads + h) * width:(heads + h + 1) * width] = out
        strided_lses.append(largest + jnp.log(sums))
        strided_deltas.append(delta_of(sdow[lines - 1, h], out))
    far_stats[0] = as_rows(strided_lses + strided_deltas)
    for j in far:
        pl.when(before(back * j))(lambda j=j: far_copy(j).start())

    for i, (to, _) in enumerate(partners):
        mxs[i] = dot_nn(att[...], w_cols(to)).astype(BF16)
        mx_copy(i).start()
    cotangent.pass_on(back)

    for h in range(heads):
        grad_p = dot_nt(dow[h, slot(0)], kvw[1, h])
        grad_s = (local_probs[h] * (grad_p - deltas[h])).astype(BF16)
        grads[0, 0, h] = (dot_nn(grad_s, kvw[0, h]) * scale).astype(BF16)
    total = dot_nn(att[...], w_cols(me))

    strided = []
    for h in range(heads):
        q, do = qkv[1, 0, h].astype(F32), sdow[lines - 1, h].astype(F32)
        delta = strided_deltas[h]
        grad_q = jnp.zeros_like(q)
        for j in [0] + far:
            prob = strided_probs[h][j]
            grad_p = jnp.sum(do * value_of(j, h), axis=1, keepdims=True)
            grad_s = (prob * (grad_p - delta)).astype(BF16).astype(F32)
            grad_q += grad_s * key_of(j, h)
            if j == 0:
                strided.append((grad_s * q, prob.astype(BF16).astype(F32) * do))
        grads[1, 0, h] = (grad_q * scale).astype(BF16)

    for d in range(1, back + 1):
        pl.when(after(d))(lambda d=d: near_copy(d).wait_recv())
    allowed = band(-ahead, after)
    for h in range(heads):
        query.finish(h)
        cotangent.finish(h)
        queries, dos, key, value = qw[h], dow[h], kvw[0, h, slot(0)], kvw[1, h, slot(0)]
        lse = jnp.concatenate([near_stats[d, h:h + 1] for d in range(back + 1)], axis=1)
        rows = [near_stats[d, heads + h:heads + h + 1] for d in range(back + 1)]
        delta = jnp.concatenate(rows, axis=1)
        probs = jnp.exp(jnp.where(allowed, dot_nt(key, queries) * scale - lse, -jnp.inf))
        grad_s = (probs * (dot_nt(value, dos) - delta)).astype(BF16)
        grads[0, 1, h] = (dot_nn(grad_s, queries) * scale).astype(BF16)
        grads[0, 2, h] = dot_nn(probs.astype(BF16), dos).astype(BF16)

    for j in far:
        @pl.when(after(back * j))
        def _(j=j):
            sq_copy(j).wait_recv()
            sdo_copy(j).wait_recv()
            far_copy(j).wait_recv()
    for j in far:
        rows = far_stats[j]
        table = jnp.concatenate([rows] * (128 // rows.shape[0]), axis=0).T
        for h in range(heads):
            q, do = sqw[j - 1, h].astype(F32), sdow[j - 1, h].astype(F32)
            lse = table[:, h:h + 1]
            delta = table[:, heads + h:heads + h + 1]
            score = jnp.sum(q * key_of(0, h), axis=1, keepdims=True) * scale
            prob = jnp.exp(jnp.where(after(back * j), score - lse, -jnp.inf))
            grad_p = jnp.sum(do * value_of(0, h), axis=1, keepdims=True)
            grad_s = (prob * (grad_p - delta)).astype(BF16).astype(F32)
            grad_k, grad_v = strided[h]
            strided[h] = (grad_k + grad_s * q, grad_v + prob.astype(BF16).astype(F32) * do)
    for h in range(heads):
        grads[1, 1, h] = (strided[h][0] * scale).astype(BF16)
        grads[1, 2, h] = strided[h][1].astype(BF16)

    for i in reversed(range(len(partners))):
        mx_copy(i).wait_recv()
        total += mxr[i].astype(F32)
    mixed[...] = total.astype(BF16)

    for i in range(len(partners)):
        og_copy(i).wait_send()
        mx_copy(i).wait_send()
    for cascade in (kv, query, cotangent):
        cascade.sent()
    for j in far:
        pl.when(after(back * j))(lambda j=j: skv_copy(j).wait_send())

        @pl.when(before(back * j))
        def _(j=j):
            sq_copy(j).wait_send()
            sdo_copy(j).wait_send()
            far_copy(j).wait_send()
    for d in range(1, back + 1):
        pl.when(before(d))(lambda d=d: near_copy(d).wait_send())


def shards(seq_count, head_groups, qkv, out_weight, out_grad):
    _, _, shard, heads, width = qkv.shape
    back = ROW // shard
    assert back * shard == ROW and back % 2 == 0 and seq_count % back == 0
    assert head_groups % 2 == 0
    lines = seq_count // back
    others = max(1, lines - 1)
    spans = list(range(1, back + 1))
    spans += [back * j for j in range(2, lines)]
    model = out_weight.shape[-1]
    cols = out_grad.shape[1]
    window = (back + 1) * shard
    stat_rows = 2 * heads
    while 128 % stat_rows or stat_rows % 8:
        stat_rows += 1
    copies = 2 * head_groups + 3 * lines + 3 * (back + 1) * heads + back + 1 + lines
    vmem = pl.BlockSpec(memory_space=pltpu.VMEM)
    hbm = pl.BlockSpec(memory_space=pltpu.HBM)
    mixed, grads = pl.pallas_call(
        functools.partial(layer_kernel, seq_count, head_groups, back, lines, spans),
        out_shape=[
            jax.ShapeDtypeStruct((shard, cols), BF16),
            jax.ShapeDtypeStruct((2, 3, heads, shard, width), BF16),
        ],
        in_specs=[pl.BlockSpec(memory_space=pl.ANY), hbm, hbm],
        out_specs=[vmem, vmem],
        scratch_shapes=[
            pltpu.VMEM((2 * heads * width, model), BF16),
            pltpu.VMEM((2, 3, heads, shard, width), BF16),
            pltpu.VMEM((shard, cols), BF16),
            pltpu.VMEM((2, heads, window, width), BF16),
            pltpu.VMEM((heads, window, width), BF16),
            pltpu.VMEM((heads, window, width), BF16),
            pltpu.VMEM((others, 2, heads, shard, width), BF16),
            pltpu.VMEM((others, heads, shard, width), BF16),
            pltpu.VMEM((lines, heads, shard, width), BF16),
            pltpu.VMEM((head_groups - 1, shard, cols), BF16),
            pltpu.VMEM((head_groups - 1, shard, cols), BF16),
            pltpu.VMEM((head_groups - 1, shard, cols), BF16),
            pltpu.VMEM((shard, 2 * heads * width), BF16),
            pltpu.VMEM((back + 1, stat_rows, shard), F32),
            pltpu.VMEM((lines, stat_rows, shard), F32),
            pltpu.SemaphoreType.DMA((5,)),
            pltpu.SemaphoreType.DMA((copies,)),
            pltpu.SemaphoreType.DMA((copies,)),
        ],
        compiler_params=pltpu.CompilerParams(
            collective_id=0, has_side_effects=True, vmem_limit_bytes=52 * 1024 * 1024
        ),
    )(
        jnp.swapaxes(qkv, 2, 3),
        out_weight.reshape(2 * heads * width, model),
        out_grad,
    )
    return mixed, jnp.swapaxes(grads, 2, 3)


def solution(mesh):
    return jax.shard_map(
        functools.partial(shards, mesh.shape["seq"], mesh.shape["head"]),
        mesh=mesh,
        in_specs=(
            P(None, None, "seq", "head", None),
            P(None, "head", None, None),
            P("seq", "head"),
        ),
        out_specs=(P("seq", "head"), P(None, None, "seq", "head", None)),
        check_vma=False,
    )
```
